256 devices in a mesh: ta: 8 (over x, core), af: 32 (over y, z).
Axes of the slice: x: 4, y: 4, z: 8, core: 2. Of those that a mesh axis runs over, the one named last changes fastest.
Arguments:
- features: bfloat16 [16, 16384, 384], P('ta', 'af'), may hold values from -6 to 6
- spatial_weights: bfloat16 [384, 1152], replicated
- spatial_output: bfloat16 [384, 384], replicated, may hold values from -0.3125 to 0.3125
- temporal_weights: bfloat16 [384, 1152], replicated
- temporal_output: bfloat16 [384, 384], replicated, may hold values from -0.3125 to 0.3125
- spatial_gain: float32 [384], replicated, may hold values from 0.1 to 1.9
- temporal_gain: float32 [384], replicated, may hold values from 0.1 to 1.9
- neighbours: int32 [128, 5], P('af'), may hold values from 0 to 127, as said below
- degrees: int32 [128], P('af'), may hold values from 2 to 5, as said below
- cotangent: bfloat16 [16, 16384, 384], P('ta', 'af'), may hold values from -6 to 6
Outputs:
- layer_output: bfloat16 [16, 16384, 384], P('ta', 'af')
- output_gradient: float32 [384, 384], P('af')
The draws below stay inside these ranges and needn't reach their ends.
Inputs may be any that keep to these rules, and one draw needn't show every extreme that they name: `neighbours`: row b lists b first, then the other node blocks that block b attends to, all distinct, within 2 blocks of b, and always including b - 1 and b + 1 where they exist; slots from degrees[b] on repeat b. degrees[b] counts the listed blocks of row b; some block has 5 and some has 2.
All inputs are finite; a program needn't handle non-finite values.
Results may differ from the reference program's by a relative error of at most 0.028.
Values may be sent and summed in bfloat16 or wider, within the bound.
A program may use at most 128 MiB of HBM per device.

```python
import jax
import jax.numpy as jnp
from jax import lax

D = 384
HEADS = 6
HDIM = 64
BLK = 128
MAXDEG = 5
WIN = 12
NBLK = 128
NODES = 16384
HOURS = 16
TOKENS = 262144


def block_lists(key):
    base = jax.random.fold_in(key, 11)
    blocks = jnp.arange(NBLK, dtype=jnp.int32)
    far_bits = jax.random.randint(base, (NBLK, 2), 0, 2).astype(jnp.int32)
    phase = blocks % 8
    far_bits = jnp.where((phase == 2)[:, None], 1, far_bits)
    far_bits = jnp.where((phase == 0)[:, None], 0, far_bits)
    offsets = jnp.array([0, -1, 1, -2, 2], dtype=jnp.int32)
    candidates = blocks[:, None] + offsets[None, :]
    inside = (candidates >= 0) & (candidates < NBLK)
    wanted = jnp.concatenate([jnp.ones((NBLK, 3), jnp.int32), far_bits], axis=1)
    chosen = inside & (wanted == 1)
    order_rank = (1 - chosen.astype(jnp.int32)) * 8 + jnp.arange(5, dtype=jnp.int32)[None, :]
    order = jnp.argsort(order_rank, axis=1)
    picked = jnp.take_along_axis(candidates, order, axis=1)
    count = jnp.sum(chosen.astype(jnp.int32), axis=1)
    slots = jnp.arange(5, dtype=jnp.int32)[None, :]
    lists = jnp.where(slots < count[:, None], picked, blocks[:, None])
    return (lists.astype(jnp.int32), count.astype(jnp.int32))


def draw_neighbours(key, part):
    return block_lists(key)[0]


def draw_degrees(key, part):
    return block_lists(key)[1]


def drawn_weights(key, salt):
    first = jax.random.truncated_normal(jax.random.fold_in(key, salt + 1), -4.0, 4.0, (D, D), jnp.float32)
    second = jax.random.truncated_normal(jax.random.fold_in(key, salt + 2), -4.0, 4.0, (D, D), jnp.float32)
    third = jax.random.truncated_normal(jax.random.fold_in(key, salt + 3), -4.0, 4.0, (D, D), jnp.float32)
    queries = first
    keys_part = second
    joined = jnp.concatenate([queries, keys_part, third], axis=1) * D ** (-0.5)
    return joined.astype(jnp.bfloat16)


def draw_spatial_weights(key, part):
    return drawn_weights(key, 100)


def draw_temporal_weights(key, part):
    return drawn_weights(key, 200)


def block_levels(own_key, dims, cuts, smallest, high):
    level = 1.0
    for dim, shards_of in cuts:
        heights = jax.random.uniform(jax.random.fold_in(jax.random.fold_in(own_key, 6), dim), (shards_of,), jnp.float32, smallest / len(cuts), high / len(cuts))
        level = level * jnp.repeat(jnp.exp(heights), dims[dim] // shards_of).reshape((-1,) + (1,) * (len(dims) - 1 - dim))
    return level


def noise(key, extent, spread, reach, cuts=(), held_as=jnp.bfloat16):
    level = block_levels(key, extent, cuts, -0.22, 0.18) if cuts else 1.0
    result = jax.random.normal(key, extent, jnp.float32) * spread * level
    return jnp.minimum(jnp.maximum(result, -reach), reach).astype(held_as)


def setup_inputs(seed: int = 0) -> dict:
    arg_keys = jax.random.split(jax.random.key(seed), 11)
    return {
        "features": noise(arg_keys[0], (HOURS, NODES, D), 1.0, 6.0, ((0, 8), (1, 32))),
        "spatial_weights": draw_spatial_weights(jax.random.fold_in(arg_keys[10], 71), 0),
        "spatial_output": noise(arg_keys[2], (D, D), D ** -0.5, 0.3125),
        "temporal_weights": draw_temporal_weights(jax.random.fold_in(arg_keys[10], 71), 0),
        "temporal_output": noise(arg_keys[4], (D, D), D ** -0.5, 0.3125),
        "spatial_gain": jnp.clip(1.0 + 0.18 * jax.random.normal(arg_keys[5], (D,), jnp.float32), 0.1, 1.9),
        "temporal_gain": jnp.clip(1.0 + 0.18 * jax.random.normal(arg_keys[6], (D,), jnp.float32), 0.1, 1.9),
        "neighbours": draw_neighbours(jax.random.fold_in(arg_keys[10], 71), 0),
        "degrees": draw_degrees(jax.random.fold_in(arg_keys[10], 71), 0),
        "cotangent": noise(arg_keys[9], (HOURS, NODES, D), 1.0, 6.0, ((0, 8), (1, 32))),
    }


def normed(inputs, gain):
    widened = inputs.astype(jnp.float32)
    mean_square = lax.optimization_barrier(jnp.mean(widened * widened, axis=-1, keepdims=True))
    return (widened * lax.rsqrt(mean_square + 1e-06) * gain).astype(jnp.bfloat16)

def soft_weights(scores, allowed):
    masked = jnp.where(allowed, scores, -1e+30)
    largest = lax.optimization_barrier(jnp.max(masked, axis=-1, keepdims=True))
    powers = jnp.where(allowed, jnp.exp(masked - largest), 0.0)
    return (powers / lax.optimization_barrier(jnp.sum(powers, axis=-1, keepdims=True))).astype(jnp.bfloat16)

def reference(features, spatial_weights, spatial_output, temporal_weights, temporal_output, spatial_gain, temporal_gain, neighbours, degrees, cotangent):
    scale = HDIM ** (-0.5)
    allowed = (jnp.arange(MAXDEG * BLK) // BLK)[None, :] < degrees[:, None]

    def spatial_hour(hour_rows):
        normed_rows = normed(hour_rows, spatial_gain)
        projected = jnp.dot(normed_rows, spatial_weights, preferred_element_type=jnp.float32).astype(jnp.bfloat16)
        queries = projected[:, :D].reshape(NBLK, BLK, HEADS, HDIM).astype(jnp.float32)
        key_value = projected[:, D:].reshape(NBLK, BLK, 2 * D)[neighbours]
        key_value = key_value.reshape(NBLK, MAXDEG * BLK, 2, HEADS, HDIM).astype(jnp.float32)
        scores = jnp.einsum('bqnd,bknd->bnqk', queries, key_value[:, :, 0]) * scale
        weights = soft_weights(scores, allowed[:, None, None, :])
        attended = jnp.einsum('bnqk,bknd->bqnd', weights.astype(jnp.float32), key_value[:, :, 1])
        attended = attended.astype(jnp.bfloat16).reshape(NODES, D)
        mixed = jnp.dot(attended, spatial_output, preferred_element_type=jnp.float32)
        return (hour_rows.astype(jnp.float32) + mixed).astype(jnp.bfloat16)
    hidden = lax.map(spatial_hour, features)
    hour_index = jnp.arange(HOURS)
    visible = (hour_index[None, :] <= hour_index[:, None]) & (hour_index[None, :] > hour_index[:, None] - WIN)
    by_block = hidden.reshape(HOURS, NBLK, BLK, D).transpose(1, 0, 2, 3)
    cot_blocks = cotangent.reshape(HOURS, NBLK, BLK, D).transpose(1, 0, 2, 3)

    def temporal_block(gradient, pieces):
        block_rows, block_cotangent = pieces
        normed_rows = normed(block_rows, temporal_gain)
        projected = jnp.dot(normed_rows.reshape(HOURS * BLK, D), temporal_weights, preferred_element_type=jnp.float32).astype(jnp.bfloat16)
        split_heads = projected.reshape(HOURS, BLK, 3, HEADS, HDIM).astype(jnp.float32)
        scores = jnp.einsum('tnhd,snhd->nhts', split_heads[:, :, 0], split_heads[:, :, 1]) * scale
        weights = soft_weights(scores, visible)
        attended = jnp.einsum('nhts,snhd->tnhd', weights.astype(jnp.float32), split_heads[:, :, 2])
        attended = attended.astype(jnp.bfloat16).reshape(HOURS * BLK, D)
        mixed = jnp.dot(attended, temporal_output, preferred_element_type=jnp.float32)
        layer_rows = (block_rows.reshape(HOURS * BLK, D).astype(jnp.float32) + mixed).astype(jnp.bfloat16)
        gradient = gradient + lax.dot_general(attended, block_cotangent.reshape(HOURS * BLK, D), (((0,), (0,)), ((), ())), preferred_element_type=jnp.float32)
        return (gradient, layer_rows.reshape(HOURS, BLK, D))
    gradient, layer_blocks = lax.scan(temporal_block, jnp.zeros((D, D), jnp.float32), (by_block, cot_blocks))
    layer_output = layer_blocks.transpose(1, 0, 2, 3).reshape(HOURS, NODES, D)
    return (layer_output, gradient * TOKENS ** (-0.5))
```

```python
import functools

import jax
import jax.numpy as jnp
from jax import lax
from jax.experimental import pallas as pl
from jax.experimental.pallas import tpu as pltpu
from jax.sharding import PartitionSpec as P

MESH = pl.DeviceIdType.MESH
F32 = jnp.float32
BF16 = jnp.bfloat16

WIDTH = 384
PAIRS = 3
BLOCK = 128
RIM = 256
SPAN = 640
WIN = 12
GROUP = 16
OWNED = 12
PADDED = 16
EXCLUDED = 1e30
SCORE_SCALE = 0.125 * 1.4426950408889634


def dot(a, b):
    return jnp.dot(a, b, preferred_element_type=F32)


def dot_nt(a, b):
    return lax.dot_general(a, b, (((1,), (1,)), ((), ())), preferred_element_type=F32)


def normed(rows, gain):
    mean_square = jnp.mean(rows * rows, axis=-1, keepdims=True)
    return (rows * lax.rsqrt(mean_square + 1e-06) * gain).astype(BF16)


def kernel(
    n_ta,
    n_af,
    tokens,
    x_ref,
    ws_ref,
    wso_ref,
    wt_ref,
    wto_ref,
    gs_ref,
    gt_ref,
    nb_ref,
    dg_ref,
    cot_ref,
    out_ref,
    grad_ref,
    halo,
    k_ext,
    q_diag,
    v_ext,
    ws_t,
    wt_t,
    staged,
    h_all,
    c_all,
    bias,
    out_staged,
    g_total,
    g_send,
    g_recv,
    t_send,
    t_recv,
    halo_send,
    halo_recv,
    c_send,
    c_recv,
    h_send,
    h_recv,
    o_send,
    o_recv,
    gs_sem,
    gr_sem,
    ts_sem,
    tr_sem,
    own_sem,
):
    ta = lax.axis_index("ta")
    af = lax.axis_index("af")
    hours_dev, nodes_dev, _ = x_ref.shape
    part = nodes_dev // n_ta
    blocks_dev = nodes_dev // BLOCK
    hours = hours_dev * n_ta
    groups = part // GROUP
    right = lax.rem(af + 1, n_af)
    left = lax.rem(af + n_af - 1, n_af)

    def to(ta_id, af_id, src, dst, send, recv):
        return pltpu.make_async_remote_copy(
            src_ref=src,
            dst_ref=dst,
            send_sem=send,
            recv_sem=recv,
            device_id=(ta_id, af_id),
            device_id_type=MESH,
        )

    def halo_right(h):
        return to(ta, right, x_ref.at[h, pl.ds(nodes_dev - RIM, RIM)], halo.at[h, 0], halo_send.at[h, 0], halo_recv.at[h, 0])

    def halo_left(h):
        return to(ta, left, x_ref.at[h, pl.ds(0, RIM)], halo.at[h, 1], halo_send.at[h, 1], halo_recv.at[h, 1])

    def cot_copy(peer, slot):
        rows = pl.ds(pl.multiple_of(peer * part, part), part)
        return to(peer, af, cot_ref.at[:, rows], c_all.at[pl.ds(slot * hours_dev, hours_dev)], c_send.at[peer], c_recv.at[slot])

    def hidden_copy(peer, h, slot):
        rows = pl.ds(pl.multiple_of(peer * part, part), part)
        return to(peer, af, staged.at[h, rows], h_all.at[slot * hours_dev + h], h_send.at[h, peer], h_recv.at[h, slot])

    def out_copy(g, peer, slot):
        rows = pl.ds(pl.multiple_of(g * GROUP, GROUP), GROUP)
        there = pl.ds(pl.multiple_of(slot * part + g * GROUP, GROUP), GROUP)
        src = out_staged.at[pl.ds(peer * hours_dev, hours_dev), rows]
        return to(peer, af, src, out_ref.at[:, there], o_send.at[g, peer], o_recv.at[g, slot])

    def grad_copy(peer, slot):
        return to(ta, peer, g_send.at[peer], g_recv.at[slot], gs_sem.at[peer], gr_sem.at[slot])

    def total_copy(peer, slot):
        return to(peer, af, t_send, t_recv.at[slot], ts_sem.at[peer], tr_sem.at[slot])

    def others(count, me, act):
        def step(i, carry):
            act(lax.rem(me + i, count))
            return carry

        lax.fori_loop(1, count, step, 0)

    barrier = pltpu.get_barrier_semaphore()
    others(n_ta, ta, lambda p: pl.semaphore_signal(barrier, inc=1, device_id=(p, af), device_id_type=MESH))
    others(n_af, af, lambda p: pl.semaphore_signal(barrier, inc=1, device_id=(ta, p), device_id_type=MESH))

    ws_t[0] = ws_ref[:, :WIDTH].T
    ws_t[1] = ws_ref[:, 2 * WIDTH :].T
    q_diag[...] = jnp.zeros_like(q_diag)
    v_ext[:, :, BLOCK:, :] = jnp.ones_like(v_ext[:, :, BLOCK:, :])

    pl.semaphore_wait(barrier, n_ta + n_af - 2)
    for h in range(hours_dev):
        halo_right(h).start()
        halo_left(h).start()
    others(n_ta, ta, lambda p: cot_copy(p, ta).start())
    own_cot = pltpu.make_async_copy(
        cot_ref.at[:, pl.ds(pl.multiple_of(ta * part, part), part)],
        c_all.at[pl.ds(ta * hours_dev, hours_dev)],
        own_sem.at[0],
    )
    own_cot.start()

    def keys_values(h, rows_normed, where):
        count = rows_normed.shape[0]
        k_ext[h, pl.ds(where, count), :] = dot(rows_normed, ws_ref[:, WIDTH : 2 * WIDTH]).astype(BF16)
        values = dot_nt(ws_t[1], rows_normed).astype(BF16)
        for pair in range(PAIRS):
            v_ext[h, pair, :BLOCK, pl.ds(where, count)] = values[pair * BLOCK : (pair + 1) * BLOCK]

    def own_rows(h, carry):
        rows = normed(x_ref[h].astype(F32), gs_ref[...])
        keys_values(h, rows, RIM)
        queries = (dot_nt(ws_t[0], rows) * SCORE_SCALE).astype(BF16)
        for pair in range(PAIRS):
            for b in range(blocks_dev):
                for k in range(2):
                    lo = k * (BLOCK // 2)
                    q_diag[h, pair, lo : lo + BLOCK // 2, (2 * b + k) * BLOCK : (2 * b + k + 1) * BLOCK] = queries[
                        pair * BLOCK + lo : pair * BLOCK + lo + BLOCK // 2, b * BLOCK : (b + 1) * BLOCK
                    ]
        return carry

    lax.fori_loop(0, hours_dev, own_rows, 0)

    wt_t[0] = wt_ref[:, :WIDTH].T
    wt_t[1] = wt_ref[:, 2 * WIDTH :].T
    key_index = lax.broadcasted_iota(jnp.int32, bias.shape, 0)
    query_index = lax.broadcasted_iota(jnp.int32, bias.shape, 1)
    ahead = query_index // GROUP - key_index // GROUP
    seen = (query_index % GROUP == key_index % GROUP) & (ahead >= 0) & (ahead < WIN)
    bias[...] = jnp.where(seen, 0.0, -EXCLUDED)
    g_total[...] = jnp.zeros_like(g_total)

    def spatial_block(h, i, carry):
        turn = jnp.where(i == 0, 2, jnp.where(i == 1, 1, jnp.where(i == 2, 3, 0)))
        b = lax.rem(ta // 2 + turn, blocks_dev)
        first = pl.multiple_of(b * BLOCK, BLOCK)
        penalty = []
        for o in range(5):
            listed = jnp.int32(0)
            for j in range(5):
                hit = (nb_ref[b, j] == af * blocks_dev + b + (o - 2)) & (j < dg_ref[b])
                listed = listed | hit.astype(jnp.int32)
            penalty.append((1 - listed).astype(F32) * EXCLUDED)
        attended = []
        for pair in range(PAIRS):
            columns = slice(pair * BLOCK, (pair + 1) * BLOCK)
            keys = k_ext[h, pl.ds(first, SPAN), columns]
            queries = q_diag[h, pair, :, pl.ds(pl.multiple_of(b * 2 * BLOCK, 2 * BLOCK), 2 * BLOCK)]
            scores = dot(keys, queries)
            tiles = [scores[o * BLOCK : (o + 1) * BLOCK] for o in range(5)]
            largest = None
            for tile, extra in zip(tiles, penalty, strict=True):
                here = jnp.max(tile, axis=0, keepdims=True) - extra
                largest = here if largest is None else jnp.maximum(largest, here)
            powers = [
                jnp.exp2(tile - (largest + extra)).astype(BF16)
                for tile, extra in zip(tiles, penalty, strict=True)
            ]
            summed = dot(v_ext[h, pair, :, pl.ds(first, SPAN)], jnp.concatenate(powers, axis=0))
            inverse = 1.0 / summed[BLOCK : BLOCK + 1]
            half = BLOCK // 2
            attended.append(summed[:half, :BLOCK] * inverse[:, :BLOCK])
            attended.append(summed[half:BLOCK, BLOCK:] * inverse[:, BLOCK:])
        attended = jnp.concatenate(attended, axis=0).T.astype(BF16)
        mixed = dot(attended, wso_ref[...])
        hidden = (x_ref[h, pl.ds(first, BLOCK)].astype(F32) + mixed).astype(BF16)
        staged[h, pl.ds(first, BLOCK)] = hidden
        for k in range(BLOCK // part):
            peer = b * (BLOCK // part) + k

            @pl.when(peer != ta)
            def _():
                hidden_copy(peer, h, ta).start()

            @pl.when(peer == ta)
            def _():
                h_all[ta * hours_dev + h] = hidden[k * part : (k + 1) * part]

        return carry

    def spatial_hour(h, carry):
        halo_right(h).wait_recv()
        halo_left(h).wait_recv()
        for side in range(2):
            rows = normed(halo[h, side].astype(F32), gs_ref[...])
            keys_values(h, rows, side * (RIM + nodes_dev))
        return lax.fori_loop(0, blocks_dev, functools.partial(spatial_block, h), carry)

    lax.fori_loop(0, hours_dev, spatial_hour, 0)

    own_cot.wait()
    others(n_ta, ta, lambda p: cot_copy(p, p).wait_recv())
    for h in range(hours_dev):
        others(n_ta, ta, lambda p, h=h: hidden_copy(p, h, p).wait_recv())

    tokens_group = hours * GROUP

    def temporal_group(g, carry):
        nodes = pl.ds(pl.multiple_of(g * GROUP, GROUP), GROUP)
        hidden = h_all[:, nodes].reshape(tokens_group, WIDTH).astype(F32)
        rows = normed(hidden, gt_ref[...])
        keys = dot(rows, wt_ref[:, WIDTH : 2 * WIDTH]).astype(BF16)
        queries = (dot_nt(wt_t[0], rows) * SCORE_SCALE).astype(BF16)
        values = dot_nt(wt_t[1], rows).astype(BF16)
        half = BLOCK // 2
        blank = jnp.zeros((half, tokens_group), BF16)
        ones = jnp.ones((PADDED, tokens_group), BF16)
        attended = []
        for head in range(2 * PAIRS):
            low = head * half
            mine = queries[low : low + half]
            padded = jnp.concatenate([mine, blank] if head % 2 == 0 else [blank, mine], axis=0)
            pair = slice(head // 2 * BLOCK, (head // 2 + 1) * BLOCK)
            scores = dot(keys[:, pair], padded) + bias[...]
            largest = jnp.max(scores, axis=0, keepdims=True)
            powers = jnp.exp2(scores - largest).astype(BF16)
            summed = dot(jnp.concatenate([values[low : low + half], ones], axis=0), powers)
            attended.append(summed[:half] * (1.0 / summed[half : half + 1]))
        attended = jnp.concatenate(attended, axis=0)
        cot = c_all[:, nodes].reshape(tokens_group, WIDTH)
        g_total[...] += dot(attended.astype(BF16), cot)
        mixed = dot(attended.T.astype(BF16), wto_ref[...])
        out_staged[:, nodes] = (hidden + mixed).astype(BF16).reshape(hours, GROUP, WIDTH)
        others(n_ta, ta, lambda p: out_copy(g, p, ta).start())
        return carry

    lax.fori_loop(0, groups, temporal_group, 0)
    own_out = pltpu.make_async_copy(
        out_staged.at[pl.ds(ta * hours_dev, hours_dev)],
        out_ref.at[:, pl.ds(pl.multiple_of(ta * part, part), part)],
        own_sem.at[1],
    )
    own_out.start()

    term = (g_total[...] * tokens ** (-0.5)).astype(BF16)
    slot = lax.broadcasted_iota(jnp.int32, (n_af * PADDED, WIDTH), 0)
    row = lax.broadcasted_iota(jnp.int32, (n_af * PADDED, WIDTH), 1)
    inside = slot % PADDED
    picks = (inside < OWNED) & (slot // PADDED * OWNED + inside == row)
    picks = jnp.where(picks, 1.0, 0.0).astype(BF16)
    g_send[...] = dot(picks, term).astype(BF16).reshape(n_af, PADDED, WIDTH)
    others(n_af, af, lambda p: grad_copy(p, af).start())
    g_recv[af] = g_send[af]
    others(n_af, af, lambda p: grad_copy(p, p).wait_recv())
    t_send[...] = jnp.sum(g_recv[...].astype(F32), axis=0)
    others(n_ta, ta, lambda p: total_copy(p, ta).start())
    t_recv[ta] = t_send[...]
    others(n_ta, ta, lambda p: total_copy(p, p).wait_recv())
    grad_ref[...] = jnp.sum(t_recv[...], axis=0)[:OWNED]

    def out_waits(g, carry):
        others(n_ta, ta, lambda p: out_copy(g, p, p).wait_recv())
        others(n_ta, ta, lambda p: out_copy(g, p, ta).wait_send())
        return carry

    lax.fori_loop(0, groups, out_waits, 0)
    own_out.wait()
    for h in range(hours_dev):
        halo_right(h).wait_send()
        halo_left(h).wait_send()
        others(n_ta, ta, lambda p, h=h: hidden_copy(p, h, ta).wait_send())
    others(n_ta, ta, lambda p: cot_copy(p, ta).wait_send())
    others(n_af, af, lambda p: grad_copy(p, af).wait_send())
    others(n_ta, ta, lambda p: total_copy(p, ta).wait_send())


def shards(n_ta, n_af, features, ws, wso, wt, wto, gain_s, gain_t, neighbours, degrees, cotangent):
    hours_dev, nodes_dev, width = features.shape
    part = nodes_dev // n_ta
    hours = hours_dev * n_ta
    groups = part // GROUP
    extended = nodes_dev + 2 * RIM
    vmem = pl.BlockSpec(memory_space=pltpu.VMEM)
    smem = pl.BlockSpec(memory_space=pltpu.SMEM)
    anywhere = pl.BlockSpec(memory_space=pl.ANY)
    dma = pltpu.SemaphoreType.DMA
    return pl.pallas_call(
        functools.partial(kernel, n_ta, n_af, hours * nodes_dev * n_af),
        out_shape=(
            jax.ShapeDtypeStruct(features.shape, BF16),
            jax.ShapeDtypeStruct((width // n_af, width), F32),
        ),
        in_specs=[vmem, vmem, vmem, vmem, vmem, vmem, vmem, smem, smem, anywhere],
        out_specs=(anywhere, vmem),
        scratch_shapes=[
            pltpu.VMEM((hours_dev, 2, RIM, width), BF16),
            pltpu.VMEM((hours_dev, extended, width), BF16),
            pltpu.VMEM((hours_dev, PAIRS, BLOCK, 2 * nodes_dev), BF16),
            pltpu.VMEM((hours_dev, PAIRS, BLOCK + PADDED, extended), BF16),
            pltpu.VMEM((2, width, width), BF16),
            pltpu.VMEM((2, width, width), BF16),
            pltpu.VMEM((hours_dev, nodes_dev, width), BF16),
            pltpu.VMEM((hours, part, width), BF16),
            pltpu.VMEM((hours, part, width), BF16),
            pltpu.VMEM((hours * GROUP, hours * GROUP), F32),
            pltpu.VMEM((hours, part, width), BF16),
            pltpu.VMEM((width, width), F32),
            pltpu.VMEM((n_af, PADDED, width), BF16),
            pltpu.VMEM((n_af, PADDED, width), BF16),
            pltpu.VMEM((PADDED, width), F32),
            pltpu.VMEM((n_ta, PADDED, width), F32),
            dma((hours_dev, 2)),
            dma((hours_dev, 2)),
            dma((n_ta,)),
            dma((n_ta,)),
            dma((hours_dev, n_ta)),
            dma((hours_dev, n_ta)),
            dma((groups, n_ta)),
            dma((groups, n_ta)),
            dma((n_af,)),
            dma((n_af,)),
            dma((n_ta,)),
            dma((n_ta,)),
            dma((2,)),
        ],
        compiler_params=pltpu.CompilerParams(
            collective_id=0, has_side_effects=True, vmem_limit_bytes=48 * 2**20
        ),
    )(features, ws, wso, wt, wto, gain_s[None], gain_t[None], neighbours, degrees, cotangent)


def solution(mesh):
    return jax.shard_map(
        functools.partial(shards, mesh.shape["ta"], mesh.shape["af"]),
        mesh=mesh,
        in_specs=(
            P("ta", "af", None),
            P(),
            P(),
            P(),
            P(),
            P(),
            P(),
            P("af", None),
            P("af"),
            P("ta", "af", None),
        ),
        out_specs=(P("ta", "af", None), P("af", None)),
        check_vma=False,
    )
```

```python
import functools

import jax
import jax.numpy as jnp
from jax import lax
from jax.experimental import pallas as pl
from jax.experimental.pallas import tpu as pltpu
from jax.sharding import PartitionSpec as P

MESH = pl.DeviceIdType.MESH
F32 = jnp.float32
BF16 = jnp.bfloat16

WIDTH = 384
PAIRS = 3
BLOCK = 128
RIM = 256
SPAN = 640
WIN = 12
GROUP = 16
OWNED = 12
PADDED = 16
EXCLUDED = 1e30
SCORE_SCALE = 0.125 * 1.4426950408889634


def dot(a, b):
    return jnp.dot(a, b, preferred_element_type=F32)


def dot_nt(a, b):
    return lax.dot_general(a, b, (((1,), (1,)), ((), ())), preferred_element_type=F32)


def normed(rows, gain):
    mean_square = jnp.mean(rows * rows, axis=-1, keepdims=True)
    return (rows * lax.rsqrt(mean_square + 1e-06) * gain).astype(BF16)


def fold(tile):
    widest = tile[:32]
    for low in range(32, tile.shape[0], 32):
        widest = jnp.maximum(widest, tile[low : low + 32])
    widest = jnp.maximum(widest[:16], widest[16:])
    return jnp.maximum(widest[:8], widest[8:])


def powers_of_two(exponents):
    return jnp.exp2(exponents.astype(BF16))


def kernel(
    n_ta,
    n_af,
    tokens,
    x_in,
    ws_in,
    wso_in,
    wt_in,
    wto_in,
    gs_in,
    gt_in,
    nb_in,
    dg_in,
    cot_ref,
    out_ref,
    grad_ref,
    x_ref,
    ws_ref,
    wso_ref,
    wt_ref,
    wto_ref,
    gs_ref,
    gt_ref,
    nb_ref,
    dg_ref,
    halo,
    k_ext,
    q_diag,
    v_ext,
    ws_t,
    wt_t,
    staged,
    h_all,
    c_all,
    bias,
    picks,
    out_staged,
    g_total,
    pair_send,
    pair_recv,
    g_send,
    g_recv,
    t_send,
    t_recv,
    halo_send,
    halo_recv,
    c_send,
    c_recv,
    h_send,
    h_recv,
    o_send,
    o_recv,
    pair_sem,
    gs_sem,
    gr_sem,
    ts_sem,
    tr_sem,
    own_sem,
    in_sem,
):
    ta = lax.axis_index("ta")
    af = lax.axis_index("af")
    hours_dev, nodes_dev, _ = x_in.shape
    part = nodes_dev // n_ta
    blocks_dev = nodes_dev // BLOCK
    hours = hours_dev * n_ta
    groups = part // GROUP
    right = lax.rem(af + 1, n_af)
    left = lax.rem(af + n_af - 1, n_af)

    def to(ta_id, af_id, src, dst, send, recv):
        return pltpu.make_async_remote_copy(
            src_ref=src,
            dst_ref=dst,
            send_sem=send,
            recv_sem=recv,
            device_id=(ta_id, af_id),
            device_id_type=MESH,
        )

    def halo_right(h):
        return to(ta, right, x_in.at[h, pl.ds(nodes_dev - RIM, RIM)], halo.at[h, 0], halo_send.at[h, 0], halo_recv.at[h, 0])

    def halo_left(h):
        return to(ta, left, x_in.at[h, pl.ds(0, RIM)], halo.at[h, 1], halo_send.at[h, 1], halo_recv.at[h, 1])

    def cot_copy(peer, slot):
        rows = pl.ds(pl.multiple_of(peer * part, part), part)
        return to(peer, af, cot_ref.at[:, rows], c_all.at[pl.ds(slot * hours_dev, hours_dev)], c_send.at[peer], c_recv.at[slot])

    def hidden_copy(peer, h, slot):
        rows = pl.ds(pl.multiple_of(peer * part, part), part)
        return to(peer, af, staged.at[h, rows], h_all.at[slot * hours_dev + h], h_send.at[h, peer], h_recv.at[h, slot])

    def out_copy(g, peer, slot):
        rows = pl.ds(pl.multiple_of(g * GROUP, GROUP), GROUP)
        there = pl.ds(pl.multiple_of(slot * part + g * GROUP, GROUP), GROUP)
        src = out_staged.at[pl.ds(peer * hours_dev, hours_dev), rows]
        return to(peer, af, src, out_ref.at[:, there], o_send.at[g, peer], o_recv.at[g, slot])

    core = lax.rem(ta, 2)
    partner = ta + 1 - 2 * core
    owners = n_af // 2
    holds = af // owners == core
    pair_copy = to(partner, af, pair_send, pair_recv, pair_sem.at[0], pair_sem.at[1])

    def grad_copy(k, owner, slot):
        return to(ta, owner, g_send.at[k], g_recv.at[slot], gs_sem.at[k], gr_sem.at[slot])

    def to_owners(act):
        def step(i, carry):
            k = lax.rem(af + i, owners)

            @pl.when(core * owners + k != af)
            def _():
                act(k)

            return carry

        lax.fori_loop(0, owners, step, 0)

    def total_copy(peer, slot):
        return to(peer, af, t_send, t_recv.at[slot], ts_sem.at[peer], tr_sem.at[slot])

    def others(count, me, act):
        def step(i, carry):
            act(lax.rem(me + i, count))
            return carry

        lax.fori_loop(1, count, step, 0)

    barrier = pltpu.get_barrier_semaphore()
    others(n_ta, ta, lambda p: pl.semaphore_signal(barrier, inc=1, device_id=(p, af), device_id_type=MESH))
    others(n_af, af, lambda p: pl.semaphore_signal(barrier, inc=1, device_id=(ta, p), device_id_type=MESH))

    loads = [
        pltpu.make_async_copy(src, dst, in_sem.at[n])
        for n, (src, dst) in enumerate(
            [
                (ws_in, ws_ref),
                (x_in, x_ref),
                (gs_in, gs_ref),
                (nb_in, nb_ref),
                (dg_in, dg_ref),
                (wso_in, wso_ref),
                (wt_in, wt_ref),
                (wto_in, wto_ref),
                (gt_in, gt_ref),
            ]
        )
    ]
    for load in loads:
        load.start()
    pl.semaphore_wait(barrier, n_ta + n_af - 2)
    halo_right(0).start()
    halo_left(0).start()
    loads[0].wait()
    ws_t[0] = ws_ref[:, :WIDTH].T
    ws_t[1] = ws_ref[:, 2 * WIDTH :].T
    q_diag[...] = jnp.zeros_like(q_diag)
    v_ext[:, :, BLOCK:, :] = jnp.ones_like(v_ext[:, :, BLOCK:, :])
    for h in range(1, hours_dev):
        halo_right(h).start()
        halo_left(h).start()
    others(n_ta, ta, lambda p: cot_copy(p, ta).start())
    own_cot = pltpu.make_async_copy(
        cot_ref.at[:, pl.ds(pl.multiple_of(ta * part, part), part)],
        c_all.at[pl.ds(ta * hours_dev, hours_dev)],
        own_sem.at[0],
    )
    own_cot.start()

    def keys_values(h, rows_normed, where):
        count = rows_normed.shape[0]
        k_ext[h, pl.ds(where, count), :] = dot(rows_normed, ws_ref[:, WIDTH : 2 * WIDTH]).astype(BF16)
        values = dot_nt(ws_t[1], rows_normed).astype(BF16)
        for pair in range(PAIRS):
            v_ext[h, pair, :BLOCK, pl.ds(where, count)] = values[pair * BLOCK : (pair + 1) * BLOCK]

    def own_rows(h, carry):
        rows = normed(x_ref[h].astype(F32), gs_ref[...][None])
        keys_values(h, rows, RIM)
        queries = (dot_nt(ws_t[0], rows) * SCORE_SCALE).astype(BF16)
        for pair in range(PAIRS):
            for b in range(blocks_dev):
                for k in range(2):
                    lo = k * (BLOCK // 2)
                    q_diag[h, pair, lo : lo + BLOCK // 2, (2 * b + k) * BLOCK : (2 * b + k + 1) * BLOCK] = queries[
                        pair * BLOCK + lo : pair * BLOCK + lo + BLOCK // 2, b * BLOCK : (b + 1) * BLOCK
                    ]
        return carry

    for load in loads[1:5]:
        load.wait()
    lax.fori_loop(0, hours_dev, own_rows, 0)
    for load in loads[5:]:
        load.wait()

    wt_t[0] = wt_ref[:, :WIDTH].T
    wt_t[1] = wt_ref[:, 2 * WIDTH :].T
    key_index = lax.broadcasted_iota(jnp.int32, bias.shape, 0)
    query_index = lax.broadcasted_iota(jnp.int32, bias.shape, 1) % BLOCK
    ahead = query_index // 8 - key_index // 8
    seen = (query_index % 8 == key_index % 8) & (ahead >= 0) & (ahead < WIN)
    bias[...] = jnp.where(seen, 0.0, -EXCLUDED)
    slot = lax.broadcasted_iota(jnp.int32, picks.shape, 0)
    row = lax.broadcasted_iota(jnp.int32, picks.shape, 1)
    inside = slot % PADDED
    wanted = (inside < OWNED) & (slot // PADDED * OWNED + inside == row)
    picks[...] = jnp.where(wanted, 1.0, 0.0).astype(BF16)
    g_total[...] = jnp.zeros_like(g_total)

    def spatial_block(h, i, carry):
        turn = jnp.where(i == 0, 2, jnp.where(i == 1, 1, jnp.where(i == 2, 3, 0)))
        b = lax.rem(ta // 2 + turn, blocks_dev)
        first = pl.multiple_of(b * BLOCK, BLOCK)
        penalty = []
        for o in range(5):
            listed = jnp.int32(0)
            for j in range(5):
                hit = (nb_ref[b, j] == af * blocks_dev + b + (o - 2)) & (j < dg_ref[b])
                listed = listed | hit.astype(jnp.int32)
            penalty.append((1 - listed).astype(F32) * EXCLUDED)
        attended = []
        for pair in range(PAIRS):
            columns = slice(pair * BLOCK, (pair + 1) * BLOCK)
            keys = k_ext[h, pl.ds(first, SPAN), columns]
            queries = q_diag[h, pair, :, pl.ds(pl.multiple_of(b * 2 * BLOCK, 2 * BLOCK), 2 * BLOCK)]
            scores = dot(keys, queries)
            tiles = [scores[o * BLOCK : (o + 1) * BLOCK] for o in range(5)]
            largest = None
            for tile, extra in zip(tiles, penalty, strict=True):
                here = fold(tile) - extra
                largest = here if largest is None else jnp.maximum(largest, here)
            largest = jnp.max(largest, axis=0, keepdims=True)
            powers = [powers_of_two(tile - (largest + extra)) for tile, extra in zip(tiles, penalty, strict=True)]
            summed = dot(v_ext[h, pair, :, pl.ds(first, SPAN)], jnp.concatenate(powers, axis=0))
            inverse = 1.0 / summed[BLOCK : BLOCK + 1]
            half = BLOCK // 2
            attended.append(summed[:half, :BLOCK] * inverse[:, :BLOCK])
            attended.append(summed[half:BLOCK, BLOCK:] * inverse[:, BLOCK:])
        attended = jnp.concatenate(attended, axis=0).T.astype(BF16)
        mixed = dot(attended, wso_ref[...])
        hidden = (x_ref[h, pl.ds(first, BLOCK)].astype(F32) + mixed).astype(BF16)
        staged[h, pl.ds(first, BLOCK)] = hidden
        for k in range(BLOCK // part):
            peer = b * (BLOCK // part) + k

            @pl.when(peer != ta)
            def _():
                hidden_copy(peer, h, ta).start()

            @pl.when(peer == ta)
            def _():
                h_all[ta * hours_dev + h] = hidden[k * part : (k + 1) * part]

        return carry

    def spatial_hour(h, carry):
        halo_right(h).wait_recv()
        halo_left(h).wait_recv()
        for side in range(2):
            rows = normed(halo[h, side].astype(F32), gs_ref[...][None])
            keys_values(h, rows, side * (RIM + nodes_dev))
        return lax.fori_loop(0, blocks_dev, functools.partial(spatial_block, h), carry)

    lax.fori_loop(0, hours_dev, spatial_hour, 0)

    own_cot.wait()
    others(n_ta, ta, lambda p: cot_copy(p, p).wait_recv())
    for h in range(hours_dev):
        others(n_ta, ta, lambda p, h=h: hidden_copy(p, h, p).wait_recv())

    def split(slab):
        return jnp.concatenate([slab[:, low : low + 8].reshape(BLOCK, WIDTH) for low in (0, 8)], axis=0)

    def joined(rows):
        return jnp.concatenate([rows[low : low + BLOCK].reshape(hours, 8, WIDTH) for low in (0, BLOCK)], axis=1)

    def temporal_group(g, carry):
        nodes = pl.ds(pl.multiple_of(g * GROUP, GROUP), GROUP)
        hidden = split(h_all[:, nodes].astype(F32))
        rows = normed(hidden, gt_ref[...][None])
        keys = dot(rows, wt_ref[:, WIDTH : 2 * WIDTH]).astype(BF16)
        queries = (dot_nt(wt_t[0], rows) * SCORE_SCALE).astype(BF16)
        values = dot_nt(wt_t[1], rows).astype(BF16)
        half = BLOCK // 2
        blank = jnp.zeros((half, BLOCK), BF16)
        ones = jnp.ones((PADDED, BLOCK), BF16)
        attended = []
        for eight in range(2):
            these = slice(eight * BLOCK, (eight + 1) * BLOCK)
            column = []
            for pair in range(PAIRS):
                heads = slice(pair * BLOCK, (pair + 1) * BLOCK)
                mine = queries[heads, these]
                diagonal = jnp.concatenate(
                    [jnp.concatenate([mine[:half], blank], axis=1), jnp.concatenate([blank, mine[half:]], axis=1)], axis=0
                )
                scores = dot(keys[these, heads], diagonal) + bias[...]
                largest = jnp.max(fold(scores), axis=0, keepdims=True)
                powers = powers_of_two(scores - largest)
                summed = dot(jnp.concatenate([values[heads, these], ones], axis=0), powers)
                inverse = 1.0 / summed[BLOCK : BLOCK + 1]
                column.append(summed[:half, :BLOCK] * inverse[:, :BLOCK])
                column.append(summed[half:BLOCK, BLOCK:] * inverse[:, BLOCK:])
            attended.append(jnp.concatenate(column, axis=0))
        cot = split(c_all[:, nodes].astype(F32)).astype(BF16)
        g_total[...] += dot(jnp.concatenate(attended, axis=1).astype(BF16), cot)
        mixed = dot(jnp.concatenate([a.T for a in attended], axis=0).astype(BF16), wto_ref[...])
        out_staged[:, nodes] = joined(hidden + mixed).astype(BF16)
        others(n_ta, ta, lambda p: out_copy(g, p, ta).start())
        return carry

    lax.fori_loop(0, groups, temporal_group, 0)
    own_out = pltpu.make_async_copy(
        out_staged.at[pl.ds(ta * hours_dev, hours_dev)],
        out_ref.at[:, pl.ds(pl.multiple_of(ta * part, part), part)],
        own_sem.at[1],
    )
    own_out.start()

    term = (g_total[...] * tokens ** (-0.5)).astype(BF16)

    def terms_of(core):
        rows = pl.ds(pl.multiple_of(core * owners * PADDED, PADDED), owners * PADDED)
        return dot(picks[rows], term).reshape(owners, PADDED, WIDTH)

    pair_send[...] = terms_of(1 - core).astype(BF16)
    pair_copy.start()
    mine = terms_of(core)
    pair_copy.wait_recv()
    g_send[...] = (mine + pair_recv[...].astype(F32)).astype(BF16)
    to_owners(lambda k: grad_copy(k, core * owners + k, af).start())

    @pl.when(holds)
    def _():
        g_recv[af] = g_send[lax.rem(af, owners)]
        others(n_af, af, lambda p: grad_copy(0, p, p).wait_recv())
        t_send[...] = jnp.sum(g_recv[...].astype(F32), axis=0)
        others(n_ta, ta, lambda p: total_copy(p, ta // 2).start())
        t_recv[ta // 2] = t_send[...]

    def holder_wait(n, carry):
        source = 2 * n + af // owners

        @pl.when(source != ta)
        def _():
            total_copy(source, n).wait_recv()

        return carry

    lax.fori_loop(0, n_ta // 2, holder_wait, 0)
    grad_ref[...] = jnp.sum(t_recv[...], axis=0)[:OWNED]

    def out_waits(g, carry):
        others(n_ta, ta, lambda p: out_copy(g, p, p).wait_recv())
        others(n_ta, ta, lambda p: out_copy(g, p, ta).wait_send())
        return carry

    lax.fori_loop(0, groups, out_waits, 0)
    own_out.wait()
    for h in range(hours_dev):
        halo_right(h).wait_send()
        halo_left(h).wait_send()
        others(n_ta, ta, lambda p, h=h: hidden_copy(p, h, ta).wait_send())
    others(n_ta, ta, lambda p: cot_copy(p, ta).wait_send())
    pair_copy.wait_send()
    to_owners(lambda k: grad_copy(k, core * owners + k, af).wait_send())

    @pl.when(holds)
    def _():
        others(n_ta, ta, lambda p: total_copy(p, ta // 2).wait_send())


def shards(n_ta, n_af, features, ws, wso, wt, wto, gain_s, gain_t, neighbours, degrees, cotangent):
    hours_dev, nodes_dev, width = features.shape
    part = nodes_dev // n_ta
    hours = hours_dev * n_ta
    groups = part // GROUP
    extended = nodes_dev + 2 * RIM
    vmem = pl.BlockSpec(memory_space=pltpu.VMEM)
    anywhere = pl.BlockSpec(memory_space=pl.ANY)
    dma = pltpu.SemaphoreType.DMA
    return pl.pallas_call(
        functools.partial(kernel, n_ta, n_af, hours * nodes_dev * n_af),
        out_shape=(
            jax.ShapeDtypeStruct(features.shape, BF16),
            jax.ShapeDtypeStruct((width // n_af, width), F32),
        ),
        in_specs=[anywhere] * 10,
        out_specs=(anywhere, vmem),
        scratch_shapes=[
            *(pltpu.VMEM(a.shape, a.dtype) for a in (features, ws, wso, wt, wto, gain_s, gain_t)),
            pltpu.SMEM(neighbours.shape, jnp.int32),
            pltpu.SMEM(degrees.shape, jnp.int32),
            pltpu.VMEM((hours_dev, 2, RIM, width), BF16),
            pltpu.VMEM((hours_dev, extended, width), BF16),
            pltpu.VMEM((hours_dev, PAIRS, BLOCK, 2 * nodes_dev), BF16),
            pltpu.VMEM((hours_dev, PAIRS, BLOCK + PADDED, extended), BF16),
            pltpu.VMEM((2, width, width), BF16),
            pltpu.VMEM((2, width, width), BF16),
            pltpu.VMEM((hours_dev, nodes_dev, width), BF16),
            pltpu.VMEM((hours, part, width), BF16),
            pltpu.VMEM((hours, part, width), BF16),
            pltpu.VMEM((BLOCK, 2 * BLOCK), F32),
            pltpu.VMEM((n_af * PADDED, width), BF16),
            pltpu.VMEM((hours, part, width), BF16),
            pltpu.VMEM((width, width), F32),
            pltpu.VMEM((n_af // 2, PADDED, width), BF16),
            pltpu.VMEM((n_af // 2, PADDED, width), BF16),
            pltpu.VMEM((n_af // 2, PADDED, width), BF16),
            pltpu.VMEM((n_af, PADDED, width), BF16),
            pltpu.VMEM((PADDED, width), F32),
            pltpu.VMEM((n_ta // 2, PADDED, width), F32),
            dma((hours_dev, 2)),
            dma((hours_dev, 2)),
            dma((n_ta,)),
            dma((n_ta,)),
            dma((hours_dev, n_ta)),
            dma((hours_dev, n_ta)),
            dma((groups, n_ta)),
            dma((groups, n_ta)),
            dma((2,)),
            dma((n_af // 2,)),
            dma((n_af,)),
            dma((n_ta,)),
            dma((n_ta // 2,)),
            dma((2,)),
            dma((9,)),
        ],
        compiler_params=pltpu.CompilerParams(
            collective_id=0, has_side_effects=True, vmem_limit_bytes=63 * 2**20
        ),
    )(features, ws, wso, wt, wto, gain_s, gain_t, neighbours, degrees, cotangent)


def solution(mesh):
    return jax.shard_map(
        functools.partial(shards, mesh.shape["ta"], mesh.shape["af"]),
        mesh=mesh,
        in_specs=(
            P("ta", "af", None),
            P(),
            P(),
            P(),
            P(),
            P(),
            P(),
            P("af", None),
            P("af"),
            P("ta", "af", None),
        ),
        out_specs=(P("ta", "af", None), P("af", None)),
        check_vma=False,
    )
```

```python
import functools

import jax
import jax.numpy as jnp
from jax import lax
from jax.experimental import pallas as pl
from jax.experimental.pallas import tpu as pltpu
from jax.sharding import PartitionSpec as P

MESH = pl.DeviceIdType.MESH
F32 = jnp.float32
BF16 = jnp.bfloat16

WIDTH = 384
HEADS = 6
HEAD = 64
PAIRS = 3
BLOCK = 128
RIM = 256
SPAN = 640
WIN = 12
TURNS = (2, 1, 3, 0)
GROUP = 16
OWNED = 12
PADDED = 16
EXCLUDED = 1e30
SCORE_SCALE = 0.125 * 1.4426950408889634


def dot(a, b):
    return jnp.dot(a, b, preferred_element_type=F32)


def dot_nt(a, b):
    return lax.dot_general(a, b, (((1,), (1,)), ((), ())), preferred_element_type=F32)


def normed(rows, gain):
    mean_square = jnp.mean(rows * rows, axis=-1, keepdims=True)
    return (rows * lax.rsqrt(mean_square + 1e-06) * gain).astype(BF16)


def fold(tile):
    widest = tile[:32]
    for low in range(32, tile.shape[0], 32):
        widest = jnp.maximum(widest, tile[low : low + 32])
    widest = jnp.maximum(widest[:16], widest[16:])
    return jnp.maximum(widest[:8], widest[8:])


def powers_of_two(exponents):
    return jnp.exp2(exponents.astype(BF16))


def staggered(units):
    count = len(units)
    for step in range(count + 2):
        if step < count:
            (scores, _, _, _), pair = units[step]
            scores(pair)
        if 0 <= step - 1 < count:
            (_, powers, _, _), pair = units[step - 1]
            powers(pair)
        if 0 <= step - 2:
            (_, _, sums, end), pair = units[step - 2]
            sums(pair)
            if pair == PAIRS - 1:
                end()


def kernel(
    n_ta,
    n_af,
    tokens,
    x_in,
    ws_in,
    wso_in,
    wt_in,
    wto_in,
    gs_in,
    gt_in,
    nb_in,
    dg_in,
    cot_ref,
    out_ref,
    grad_ref,
    x_ref,
    ws_ref,
    wso_ref,
    wt_ref,
    wto_ref,
    gs_ref,
    gt_ref,
    nb_ref,
    dg_ref,
    halo,
    k_ext,
    q_diag,
    v_ext,
    ws_t,
    wt_t,
    staged,
    h_all,
    c_all,
    bias,
    picks,
    out_staged,
    g_total,
    pair_send,
    pair_recv,
    g_send,
    g_recv,
    t_send,
    t_recv,
    halo_send,
    halo_recv,
    c_send,
    c_recv,
    h_send,
    h_recv,
    o_send,
    o_recv,
    pair_sem,
    gs_sem,
    gr_sem,
    ts_sem,
    tr_sem,
    own_sem,
    in_sem,
):
    ta = lax.axis_index("ta")
    af = lax.axis_index("af")
    hours_dev, nodes_dev, _ = x_in.shape
    part = nodes_dev // n_ta
    blocks_dev = nodes_dev // BLOCK
    hours = hours_dev * n_ta
    groups = part // GROUP
    right = lax.rem(af + 1, n_af)
    left = lax.rem(af + n_af - 1, n_af)

    def to(ta_id, af_id, src, dst, send, recv):
        return pltpu.make_async_remote_copy(
            src_ref=src,
            dst_ref=dst,
            send_sem=send,
            recv_sem=recv,
            device_id=(ta_id, af_id),
            device_id_type=MESH,
        )

    def halo_right(h):
        return to(ta, right, x_in.at[h, pl.ds(nodes_dev - RIM, RIM)], halo.at[h, 0], halo_send.at[h, 0], halo_recv.at[h, 0])

    def halo_left(h):
        return to(ta, left, x_in.at[h, pl.ds(0, RIM)], halo.at[h, 1], halo_send.at[h, 1], halo_recv.at[h, 1])

    def cot_copy(peer, slot):
        rows = pl.ds(pl.multiple_of(peer * part, part), part)
        return to(peer, af, cot_ref.at[:, rows], c_all.at[pl.ds(slot * hours_dev, hours_dev)], c_send.at[peer], c_recv.at[slot])

    def hidden_copy(peer, h, slot):
        rows = pl.ds(pl.multiple_of(peer * part, part), part)
        return to(peer, af, staged.at[h, rows], h_all.at[slot * hours_dev + h], h_send.at[h, peer], h_recv.at[h, slot])

    def out_copy(g, peer, slot):
        rows = pl.ds(pl.multiple_of(g * GROUP, GROUP), GROUP)
        there = pl.ds(pl.multiple_of(slot * part + g * GROUP, GROUP), GROUP)
        src = out_staged.at[pl.ds(peer * hours_dev, hours_dev), rows]
        return to(peer, af, src, out_ref.at[:, there], o_send.at[g, peer], o_recv.at[g, slot])

    core = lax.rem(ta, 2)
    partner = ta + 1 - 2 * core
    owners = n_af // 2
    holds = af // owners == core
    pair_copy = to(partner, af, pair_send, pair_recv, pair_sem.at[0], pair_sem.at[1])

    def grad_copy(k, owner, slot):
        return to(ta, owner, g_send.at[k], g_recv.at[slot], gs_sem.at[k], gr_sem.at[slot])

    def to_owners(act):
        def step(i, carry):
            k = lax.rem(af + i, owners)

            @pl.when(core * owners + k != af)
            def _():
                act(k)

            return carry

        lax.fori_loop(0, owners, step, 0)

    def total_copy(peer, slot):
        return to(peer, af, t_send, t_recv.at[slot], ts_sem.at[peer], tr_sem.at[slot])

    def others(count, me, act):
        def step(i, carry):
            act(lax.rem(me + i, count))
            return carry

        lax.fori_loop(1, count, step, 0)

    barrier = pltpu.get_barrier_semaphore()
    others(n_ta, ta, lambda p: pl.semaphore_signal(barrier, inc=1, device_id=(p, af), device_id_type=MESH))
    others(n_af, af, lambda p: pl.semaphore_signal(barrier, inc=1, device_id=(ta, p), device_id_type=MESH))

    loads = [
        pltpu.make_async_copy(src, dst, in_sem.at[n])
        for n, (src, dst) in enumerate(
            [
                (ws_in, ws_ref),
                (x_in, x_ref),
                (gs_in, gs_ref),
                (nb_in, nb_ref),
                (dg_in, dg_ref),
                (wso_in, wso_ref),
                (wt_in, wt_ref),
                (wto_in, wto_ref),
                (gt_in, gt_ref),
            ]
        )
    ]
    for load in loads:
        load.start()
    pl.semaphore_wait(barrier, n_ta + n_af - 2)
    halo_right(0).start()
    halo_left(0).start()
    loads[0].wait()
    ws_t[0] = ws_ref[:, :WIDTH].T
    ws_t[1] = ws_ref[:, 2 * WIDTH :].T
    q_diag[...] = jnp.zeros_like(q_diag)
    v_ext[:, :, HEAD:, :] = jnp.ones_like(v_ext[:, :, HEAD:, :])
    for h in range(1, hours_dev):
        halo_right(h).start()
        halo_left(h).start()
    others(n_ta, ta, lambda p: cot_copy(p, ta).start())
    own_cot = pltpu.make_async_copy(
        cot_ref.at[:, pl.ds(pl.multiple_of(ta * part, part), part)],
        c_all.at[pl.ds(ta * hours_dev, hours_dev)],
        own_sem.at[0],
    )
    own_cot.start()

    def keys_values(h, rows_normed, where):
        count = rows_normed.shape[0]
        k_ext[h, pl.ds(where, count), :] = dot(rows_normed, ws_ref[:, WIDTH : 2 * WIDTH]).astype(BF16)
        values = dot_nt(ws_t[1], rows_normed).astype(BF16)
        for head in range(HEADS):
            v_ext[h, head, :HEAD, pl.ds(where, count)] = values[head * HEAD : (head + 1) * HEAD]

    def own_rows(h, carry):
        rows = normed(x_ref[h].astype(F32), gs_ref[...][None])
        keys_values(h, rows, RIM)
        queries = (dot_nt(ws_t[0], rows) * SCORE_SCALE).astype(BF16)
        for pair in range(PAIRS):
            for b in range(blocks_dev):
                for k in range(2):
                    lo = k * (BLOCK // 2)
                    q_diag[h, pair, lo : lo + BLOCK // 2, (2 * b + k) * BLOCK : (2 * b + k + 1) * BLOCK] = queries[
                        pair * BLOCK + lo : pair * BLOCK + lo + BLOCK // 2, b * BLOCK : (b + 1) * BLOCK
                    ]
        return carry

    for load in loads[1:5]:
        load.wait()
    lax.fori_loop(0, hours_dev, own_rows, 0)
    for load in loads[5:]:
        load.wait()

    wt_t[0] = wt_ref[:, :WIDTH].T
    wt_t[1] = wt_ref[:, 2 * WIDTH :].T
    key_index = lax.broadcasted_iota(jnp.int32, bias.shape, 0)
    query_index = lax.broadcasted_iota(jnp.int32, bias.shape, 1) % BLOCK
    ahead = query_index // 8 - key_index // 8
    seen = (query_index % 8 == key_index % 8) & (ahead >= 0) & (ahead < WIN)
    bias[...] = jnp.where(seen, 0.0, -EXCLUDED)
    slot = lax.broadcasted_iota(jnp.int32, picks.shape, 0)
    row = lax.broadcasted_iota(jnp.int32, picks.shape, 1)
    inside = slot % PADDED
    wanted = (inside < OWNED) & (slot // PADDED * OWNED + inside == row)
    picks[...] = jnp.where(wanted, 1.0, 0.0).astype(BF16)
    g_total[...] = jnp.zeros_like(g_total)

    def spatial_turn(h, turn):
        b = lax.rem(ta // 2 + TURNS[turn], blocks_dev)
        first = pl.multiple_of(b * BLOCK, BLOCK)
        penalty = []
        for o in range(5):
            listed = jnp.int32(0)
            for j in range(5):
                hit = (nb_ref[b, j] == af * blocks_dev + b + (o - 2)) & (j < dg_ref[b])
                listed = listed | hit.astype(jnp.int32)
            penalty.append((1 - listed).astype(F32) * EXCLUDED)
        cuts = (((0, 128, 0), (128, 256, 1), (256, 320, 2)), ((0, 64, 2), (64, 192, 3), (192, 320, 4)))
        held = {}
        attended = []

        def scores(pair):
            columns = slice(pair * BLOCK, (pair + 1) * BLOCK)
            queries = q_diag[h, pair, :, pl.ds(pl.multiple_of(b * 2 * BLOCK, 2 * BLOCK), 2 * BLOCK)]
            tiles = []
            for part_of, cut in enumerate(cuts):
                start = pl.multiple_of(first + part_of * (SPAN // 2), HEAD)
                product = dot(k_ext[h, pl.ds(start, SPAN // 2), columns], queries)
                tiles += [(product[low:high], penalty[o]) for low, high, o in cut]
            largest = functools.reduce(jnp.maximum, [fold(tile) - extra for tile, extra in tiles])
            held[pair] = tiles, jnp.max(largest, axis=0, keepdims=True)

        def powers(pair):
            tiles, largest = held[pair]
            held[pair] = jnp.concatenate([powers_of_two(tile - (largest + extra)) for tile, extra in tiles], axis=0)

        def sums(pair):
            weights = held.pop(pair)
            for k in range(2):
                summed = dot(v_ext[h, 2 * pair + k, :, pl.ds(first, SPAN)], weights[:, k * BLOCK : (k + 1) * BLOCK])
                attended.append(summed[:HEAD] * (1.0 / summed[HEAD : HEAD + 1]))

        def end():
            rows = jnp.concatenate(attended, axis=0).T.astype(BF16)
            mixed = dot(rows, wso_ref[...])
            hidden = (x_ref[h, pl.ds(first, BLOCK)].astype(F32) + mixed).astype(BF16)
            staged[h, pl.ds(first, BLOCK)] = hidden
            if TURNS[turn]:
                for k in range(2):
                    hidden_copy(2 * b + k, h, ta).start()
            else:
                hidden_copy(partner, h, ta).start()
                mine = pl.ds(pl.multiple_of(ta * part, part), part)
                h_all[ta * hours_dev + h] = staged[h, mine]

        return scores, powers, sums, end

    def spatial_hour(h, carry):
        halo_right(h).wait_recv()
        halo_left(h).wait_recv()
        for side in range(2):
            rows = normed(halo[h, side].astype(F32), gs_ref[...][None])
            keys_values(h, rows, side * (RIM + nodes_dev))
        turns = [spatial_turn(h, turn) for turn in range(blocks_dev)]
        units = [(turn, pair) for turn in turns for pair in range(PAIRS)]
        staggered(units)
        return carry

    lax.fori_loop(0, hours_dev, spatial_hour, 0)

    own_cot.wait()
    others(n_ta, ta, lambda p: cot_copy(p, p).wait_recv())
    for h in range(hours_dev):
        others(n_ta, ta, lambda p, h=h: hidden_copy(p, h, p).wait_recv())

    def split(slab):
        return jnp.concatenate([slab[:, low : low + 8].reshape(BLOCK, WIDTH) for low in (0, 8)], axis=0)

    def joined(rows):
        return jnp.concatenate([rows[low : low + BLOCK].reshape(hours, 8, WIDTH) for low in (0, BLOCK)], axis=1)

    def temporal_group(g, carry):
        nodes = pl.ds(pl.multiple_of(g * GROUP, GROUP), GROUP)
        hidden = split(h_all[:, nodes].astype(F32))
        rows = normed(hidden, gt_ref[...][None])
        keys = dot(rows, wt_ref[:, WIDTH : 2 * WIDTH]).astype(BF16)
        queries = (dot_nt(wt_t[0], rows) * SCORE_SCALE).astype(BF16)
        values = dot_nt(wt_t[1], rows).astype(BF16)
        blank = jnp.zeros((HEAD, BLOCK), BF16)
        ones = jnp.ones((PADDED, BLOCK), BF16)
        attended = []

        def eight_nodes(eight):
            these = slice(eight * BLOCK, (eight + 1) * BLOCK)
            held = {}
            column = []

            def scores(pair):
                heads = slice(pair * BLOCK, (pair + 1) * BLOCK)
                mine = queries[heads, these]
                diagonal = jnp.concatenate(
                    [jnp.concatenate([mine[:HEAD], blank], axis=1), jnp.concatenate([blank, mine[HEAD:]], axis=1)], axis=0
                )
                product = dot(keys[these, heads], diagonal) + bias[...]
                held[pair] = product, jnp.max(fold(product), axis=0, keepdims=True)

            def powers(pair):
                product, largest = held[pair]
                held[pair] = powers_of_two(product - largest)

            def sums(pair):
                weights = held.pop(pair)
                for k in range(2):
                    low = (2 * pair + k) * HEAD
                    summed = dot(
                        jnp.concatenate([values[low : low + HEAD, these], ones], axis=0),
                        weights[:, k * BLOCK : (k + 1) * BLOCK],
                    )
                    column.append(summed[:HEAD] * (1.0 / summed[HEAD : HEAD + 1]))

            def end():
                attended.append(jnp.concatenate(column, axis=0))

            return scores, powers, sums, end

        sets = [eight_nodes(eight) for eight in range(2)]
        staggered([(nodes_set, pair) for nodes_set in sets for pair in range(PAIRS)])
        cot = split(c_all[:, nodes].astype(F32)).astype(BF16)
        g_total[...] += dot(jnp.concatenate(attended, axis=1).astype(BF16), cot)
        mixed = dot(jnp.concatenate([a.T for a in attended], axis=0).astype(BF16), wto_ref[...])
        out_staged[:, nodes] = joined(hidden + mixed).astype(BF16)
        for i in range(1, n_ta):
            out_copy(g, lax.rem(ta + i, n_ta), ta).start()
        return carry

    lax.fori_loop(0, groups, temporal_group, 0)
    own_out = pltpu.make_async_copy(
        out_staged.at[pl.ds(ta * hours_dev, hours_dev)],
        out_ref.at[:, pl.ds(pl.multiple_of(ta * part, part), part)],
        own_sem.at[1],
    )
    own_out.start()

    term = (g_total[...] * tokens ** (-0.5)).astype(BF16)

    def terms_of(core):
        rows = pl.ds(pl.multiple_of(core * owners * PADDED, PADDED), owners * PADDED)
        return dot(picks[rows], term).reshape(owners, PADDED, WIDTH)

    pair_send[...] = terms_of(1 - core).astype(BF16)
    pair_copy.start()
    mine = terms_of(core)
    pair_copy.wait_recv()
    g_send[...] = (mine + pair_recv[...].astype(F32)).astype(BF16)
    to_owners(lambda k: grad_copy(k, core * owners + k, af).start())

    @pl.when(holds)
    def _():
        g_recv[af] = g_send[lax.rem(af, owners)]
        others(n_af, af, lambda p: grad_copy(0, p, p).wait_recv())
        t_send[...] = jnp.sum(g_recv[...].astype(F32), axis=0)
        others(n_ta, ta, lambda p: total_copy(p, ta // 2).start())
        t_recv[ta // 2] = t_send[...]

    def holder_wait(n, carry):
        source = 2 * n + af // owners

        @pl.when(source != ta)
        def _():
            total_copy(source, n).wait_recv()

        return carry

    lax.fori_loop(0, n_ta // 2, holder_wait, 0)
    grad_ref[...] = t_recv[...]

    def out_waits(g, carry):
        others(n_ta, ta, lambda p: out_copy(g, p, p).wait_recv())
        others(n_ta, ta, lambda p: out_copy(g, p, ta).wait_send())
        return carry

    lax.fori_loop(0, groups, out_waits, 0)
    own_out.wait()
    for h in range(hours_dev):
        halo_right(h).wait_send()
        halo_left(h).wait_send()
        others(n_ta, ta, lambda p, h=h: hidden_copy(p, h, ta).wait_send())
    others(n_ta, ta, lambda p: cot_copy(p, ta).wait_send())
    pair_copy.wait_send()
    to_owners(lambda k: grad_copy(k, core * owners + k, af).wait_send())

    @pl.when(holds)
    def _():
        others(n_ta, ta, lambda p: total_copy(p, ta // 2).wait_send())


def closing(pieces, made_ref, terms_ref, out_ref, grad_ref, sems):
    hours_dev, nodes_dev, _ = made_ref.shape
    size = nodes_dev // pieces
    copies = [
        pltpu.make_async_copy(
            made_ref.at[h, pl.ds(n * size, size)], out_ref.at[h, pl.ds(n * size, size)], sems.at[h, n]
        )
        for h in range(hours_dev)
        for n in range(pieces)
    ]
    for copy in copies:
        copy.start()
    grad_ref[...] = jnp.sum(terms_ref[...], axis=0)[:OWNED]
    for copy in copies:
        copy.wait()


def shards(n_ta, n_af, features, ws, wso, wt, wto, gain_s, gain_t, neighbours, degrees, cotangent):
    hours_dev, nodes_dev, width = features.shape
    part = nodes_dev // n_ta
    hours = hours_dev * n_ta
    groups = part // GROUP
    extended = nodes_dev + 2 * RIM
    vmem = pl.BlockSpec(memory_space=pltpu.VMEM)
    anywhere = pl.BlockSpec(memory_space=pl.ANY)
    dma = pltpu.SemaphoreType.DMA
    output, terms = pl.pallas_call(
        functools.partial(kernel, n_ta, n_af, hours * nodes_dev * n_af),
        out_shape=(
            jax.ShapeDtypeStruct(features.shape, BF16),
            jax.ShapeDtypeStruct((n_ta // 2, PADDED, width), F32),
        ),
        in_specs=[anywhere] * 10,
        out_specs=(anywhere, vmem),
        scratch_shapes=[
            *(pltpu.VMEM(a.shape, a.dtype) for a in (features, ws, wso, wt, wto, gain_s, gain_t)),
            pltpu.SMEM(neighbours.shape, jnp.int32),
            pltpu.SMEM(degrees.shape, jnp.int32),
            pltpu.VMEM((hours_dev, 2, RIM, width), BF16),
            pltpu.VMEM((hours_dev, extended, width), BF16),
            pltpu.VMEM((hours_dev, PAIRS, BLOCK, 2 * nodes_dev), BF16),
            pltpu.VMEM((hours_dev, HEADS, HEAD + PADDED, extended), BF16),
            pltpu.VMEM((2, width, width), BF16),
            pltpu.VMEM((2, width, width), BF16),
            pltpu.VMEM((hours_dev, nodes_dev, width), BF16),
            pltpu.VMEM((hours, part, width), BF16),
            pltpu.VMEM((hours, part, width), BF16),
            pltpu.VMEM((BLOCK, 2 * BLOCK), F32),
            pltpu.VMEM((n_af * PADDED, width), BF16),
            pltpu.VMEM((hours, part, width), BF16),
            pltpu.VMEM((width, width), F32),
            pltpu.VMEM((n_af // 2, PADDED, width), BF16),
            pltpu.VMEM((n_af // 2, PADDED, width), BF16),
            pltpu.VMEM((n_af // 2, PADDED, width), BF16),
            pltpu.VMEM((n_af, PADDED, width), BF16),
            pltpu.VMEM((PADDED, width), F32),
            pltpu.VMEM((n_ta // 2, PADDED, width), F32),
            dma((hours_dev, 2)),
            dma((hours_dev, 2)),
            dma((n_ta,)),
            dma((n_ta,)),
            dma((hours_dev, n_ta)),
            dma((hours_dev, n_ta)),
            dma((groups, n_ta)),
            dma((groups, n_ta)),
            dma((2,)),
            dma((n_af // 2,)),
            dma((n_af,)),
            dma((n_ta,)),
            dma((n_ta // 2,)),
            dma((2,)),
            dma((9,)),
        ],
        compiler_params=pltpu.CompilerParams(
            collective_id=0, has_side_effects=True, vmem_limit_bytes=63 * 2**20
        ),
    )(features, ws, wso, wt, wto, gain_s, gain_t, neighbours, degrees, cotangent)
    pieces = 8
    return pl.pallas_call(
        functools.partial(closing, pieces),
        out_shape=(
            jax.ShapeDtypeStruct(features.shape, BF16),
            jax.ShapeDtypeStruct((width // n_af, width), F32),
        ),
        in_specs=[anywhere, vmem],
        out_specs=(anywhere, vmem),
        scratch_shapes=[dma((hours_dev, pieces))],
        compiler_params=pltpu.CompilerParams(vmem_limit_bytes=63 * 2**20),
    )(output, terms)


def solution(mesh):
    return jax.shard_map(
        functools.partial(shards, mesh.shape["ta"], mesh.shape["af"]),
        mesh=mesh,
        in_specs=(
            P("ta", "af", None),
            P(),
            P(),
            P(),
            P(),
            P(),
            P(),
            P("af", None),
            P("af"),
            P("ta", "af", None),
        ),
        out_specs=(P("ta", "af", None), P("af", None)),
        check_vma=False,
    )
```

```python
import functools

import jax
import jax.numpy as jnp
from jax import lax
from jax.experimental import pallas as pl
from jax.experimental.pallas import tpu as pltpu
from jax.sharding import PartitionSpec as P

MESH = pl.DeviceIdType.MESH
F32 = jnp.float32
BF16 = jnp.bfloat16

WIDTH = 384
HEADS = 6
HEAD = 64
PAIRS = 3
BLOCK = 128
RIM = 256
SPAN = 640
WIN = 12
TURNS = (2, 1, 3, 0)
GROUP = 16
OWNED = 12
PADDED = 16
EXCLUDED = 1e30
SCORE_SCALE = 0.125 * 1.4426950408889634


def dot(a, b):
    return jnp.dot(a, b, preferred_element_type=F32)


def dot_nt(a, b):
    return lax.dot_general(a, b, (((1,), (1,)), ((), ())), preferred_element_type=F32)


def normed(rows, gain):
    mean_square = jnp.mean(rows * rows, axis=-1, keepdims=True)
    return (rows * lax.rsqrt(mean_square + 1e-06) * gain).astype(BF16)


def fold(tile):
    widest = tile[:32]
    for low in range(32, tile.shape[0], 32):
        widest = jnp.maximum(widest, tile[low : low + 32])
    widest = jnp.maximum(widest[:16], widest[16:])
    return jnp.maximum(widest[:8], widest[8:])


def powers_of_two(exponents):
    return jnp.exp2(exponents.astype(BF16))


def staggered(units):
    count = len(units)
    for step in range(count + 2):
        if step < count:
            (scores, _, _, _), pair = units[step]
            scores(pair)
        if 0 <= step - 1 < count:
            (_, powers, _, _), pair = units[step - 1]
            powers(pair)
        if 0 <= step - 2:
            (_, _, sums, end), pair = units[step - 2]
            sums(pair)
            if pair == PAIRS - 1:
                end()


def kernel(
    n_ta,
    n_af,
    tokens,
    x_in,
    ws_in,
    wso_in,
    wt_in,
    wto_in,
    gs_in,
    gt_in,
    nb_in,
    dg_in,
    cot_ref,
    out_ref,
    grad_ref,
    x_ref,
    ws_ref,
    wso_ref,
    wt_ref,
    wto_ref,
    gs_ref,
    gt_ref,
    nb_ref,
    dg_ref,
    halo,
    k_ext,
    q_diag,
    v_ext,
    ws_t,
    wt_t,
    staged,
    h_all,
    c_all,
    bias,
    picks,
    out_staged,
    g_total,
    pair_send,
    pair_recv,
    g_send,
    g_recv,
    t_send,
    t_recv,
    halo_send,
    halo_recv,
    c_send,
    c_recv,
    h_send,
    h_recv,
    o_send,
    o_recv,
    pair_sem,
    gs_sem,
    gr_sem,
    ts_sem,
    tr_sem,
    own_sem,
    in_sem,
):
    ta = lax.axis_index("ta")
    af = lax.axis_index("af")
    hours_dev, nodes_dev, _ = x_in.shape
    part = nodes_dev // n_ta
    blocks_dev = nodes_dev // BLOCK
    hours = hours_dev * n_ta
    groups = part // GROUP
    right = lax.rem(af + 1, n_af)
    left = lax.rem(af + n_af - 1, n_af)

    def to(ta_id, af_id, src, dst, send, recv):
        return pltpu.make_async_remote_copy(
            src_ref=src,
            dst_ref=dst,
            send_sem=send,
            recv_sem=recv,
            device_id=(ta_id, af_id),
            device_id_type=MESH,
        )

    def halo_right(h):
        return to(ta, right, x_in.at[h, pl.ds(nodes_dev - RIM, RIM)], halo.at[h, 0], halo_send.at[h, 0], halo_recv.at[h, 0])

    def halo_left(h):
        return to(ta, left, x_in.at[h, pl.ds(0, RIM)], halo.at[h, 1], halo_send.at[h, 1], halo_recv.at[h, 1])

    def cot_copy(peer, slot):
        rows = pl.ds(pl.multiple_of(peer * part, part), part)
        return to(peer, af, cot_ref.at[:, rows], c_all.at[pl.ds(slot * hours_dev, hours_dev)], c_send.at[peer], c_recv.at[slot])

    def hidden_copy(peer, h, slot):
        rows = pl.ds(pl.multiple_of(peer * part, part), part)
        return to(peer, af, staged.at[h, rows], h_all.at[slot * hours_dev + h], h_send.at[h, peer], h_recv.at[h, slot])

    def out_copy(g, peer, slot):
        rows = pl.ds(pl.multiple_of(g * GROUP, GROUP), GROUP)
        there = pl.ds(pl.multiple_of(slot * part + g * GROUP, GROUP), GROUP)
        src = out_staged.at[pl.ds(peer * hours_dev, hours_dev), rows]
        return to(peer, af, src, out_ref.at[:, there], o_send.at[g, peer], o_recv.at[g, slot])

    core = lax.rem(ta, 2)
    partner = ta + 1 - 2 * core
    owners = n_af // 2
    holds = af // owners == core
    pair_copy = to(partner, af, pair_send, pair_recv, pair_sem.at[0], pair_sem.at[1])

    def grad_copy(k, owner, slot):
        return to(ta, owner, g_send.at[k], g_recv.at[slot], gs_sem.at[k], gr_sem.at[slot])

    def to_owners(act):
        def step(i, carry):
            k = lax.rem(af + i, owners)

            @pl.when(core * owners + k != af)
            def _():
                act(k)

            return carry

        lax.fori_loop(0, owners, step, 0)

    def total_copy(peer, slot):
        return to(peer, af, t_send, t_recv.at[slot], ts_sem.at[peer], tr_sem.at[slot])

    def others(count, me, act):
        def step(i, carry):
            act(lax.rem(me + i, count))
            return carry

        lax.fori_loop(1, count, step, 0)

    barrier = pltpu.get_barrier_semaphore()
    others(n_ta, ta, lambda p: pl.semaphore_signal(barrier, inc=1, device_id=(p, af), device_id_type=MESH))
    others(n_af, af, lambda p: pl.semaphore_signal(barrier, inc=1, device_id=(ta, p), device_id_type=MESH))

    loads = [
        pltpu.make_async_copy(src, dst, in_sem.at[n])
        for n, (src, dst) in enumerate(
            [
                (ws_in, ws_ref),
                (x_in, x_ref),
                (gs_in, gs_ref),
                (nb_in, nb_ref),
                (dg_in, dg_ref),
                (wso_in, wso_ref),
                (wt_in, wt_ref),
                (wto_in, wto_ref),
                (gt_in, gt_ref),
            ]
        )
    ]
    for load in loads:
        load.start()
    pl.semaphore_wait(barrier, n_ta + n_af - 2)
    halo_right(0).start()
    halo_left(0).start()
    loads[0].wait()
    ws_t[0] = ws_ref[:, :WIDTH].T
    ws_t[1] = ws_ref[:, 2 * WIDTH :].T
    q_diag[...] = jnp.zeros_like(q_diag)
    v_ext[:, :, HEAD:, :] = jnp.ones_like(v_ext[:, :, HEAD:, :])
    for h in range(1, hours_dev):
        halo_right(h).start()
        halo_left(h).start()
    others(n_ta, ta, lambda p: cot_copy(p, ta).start())
    own_cot = pltpu.make_async_copy(
        cot_ref.at[:, pl.ds(pl.multiple_of(ta * part, part), part)],
        c_all.at[pl.ds(ta * hours_dev, hours_dev)],
        own_sem.at[0],
    )
    own_cot.start()

    def keys_values(h, rows_normed, where):
        count = rows_normed.shape[0]
        k_ext[h, pl.ds(where, count), :] = dot(rows_normed, ws_ref[:, WIDTH : 2 * WIDTH]).astype(BF16)
        values = dot_nt(ws_t[1], rows_normed).astype(BF16)
        for head in range(HEADS):
            v_ext[h, head, :HEAD, pl.ds(where, count)] = values[head * HEAD : (head + 1) * HEAD]

    def own_rows(h, carry):
        rows = normed(x_ref[h].astype(F32), gs_ref[...][None])
        keys_values(h, rows, RIM)
        queries = (dot_nt(ws_t[0], rows) * SCORE_SCALE).astype(BF16)
        for pair in range(PAIRS):
            for b in range(blocks_dev):
                for k in range(2):
                    lo = k * (BLOCK // 2)
                    q_diag[h, pair, lo : lo + BLOCK // 2, (2 * b + k) * BLOCK : (2 * b + k + 1) * BLOCK] = queries[
                        pair * BLOCK + lo : pair * BLOCK + lo + BLOCK // 2, b * BLOCK : (b + 1) * BLOCK
                    ]
        return carry

    for load in loads[1:5]:
        load.wait()
    lax.fori_loop(0, hours_dev, own_rows, 0)
    for load in loads[5:]:
        load.wait()

    wt_t[0] = wt_ref[:, :WIDTH].T
    wt_t[1] = wt_ref[:, 2 * WIDTH :].T
    key_index = lax.broadcasted_iota(jnp.int32, bias.shape, 0)
    query_index = lax.broadcasted_iota(jnp.int32, bias.shape, 1) % BLOCK
    ahead = query_index // 8 - key_index // 8
    seen = (query_index % 8 == key_index % 8) & (ahead >= 0) & (ahead < WIN)
    bias[...] = jnp.where(seen, 0.0, -EXCLUDED)
    slot = lax.broadcasted_iota(jnp.int32, picks.shape, 0)
    row = lax.broadcasted_iota(jnp.int32, picks.shape, 1)
    inside = slot % PADDED
    wanted = (inside < OWNED) & (slot // PADDED * OWNED + inside == row)
    picks[...] = jnp.where(wanted, 1.0, 0.0).astype(BF16)
    g_total[...] = jnp.zeros_like(g_total)

    def spatial_turn(h, turn):
        b = lax.rem(ta // 2 + TURNS[turn], blocks_dev)
        first = pl.multiple_of(b * BLOCK, BLOCK)
        penalty = []
        for o in range(5):
            listed = jnp.int32(0)
            for j in range(5):
                hit = (nb_ref[b, j] == af * blocks_dev + b + (o - 2)) & (j < dg_ref[b])
                listed = listed | hit.astype(jnp.int32)
            penalty.append((1 - listed).astype(F32) * EXCLUDED)
        cuts = (((0, 128, 0), (128, 256, 1), (256, 320, 2)), ((0, 64, 2), (64, 192, 3), (192, 320, 4)))
        held = {}
        attended = []

        def scores(pair):
            columns = slice(pair * BLOCK, (pair + 1) * BLOCK)
            queries = q_diag[h, pair, :, pl.ds(pl.multiple_of(b * 2 * BLOCK, 2 * BLOCK), 2 * BLOCK)]
            tiles = []
            for part_of, cut in enumerate(cuts):
                start = pl.multiple_of(first + part_of * (SPAN // 2), HEAD)
                product = dot(k_ext[h, pl.ds(start, SPAN // 2), columns], queries)
                tiles += [(product[low:high], penalty[o]) for low, high, o in cut]
            largest = functools.reduce(jnp.maximum, [fold(tile) - extra for tile, extra in tiles])
            held[pair] = tiles, jnp.max(largest, axis=0, keepdims=True)

        def powers(pair):
            tiles, largest = held[pair]
            held[pair] = jnp.concatenate([powers_of_two(tile - (largest + extra)) for tile, extra in tiles], axis=0)

        def sums(pair):
            weights = held.pop(pair)
            for k in range(2):
                summed = dot(v_ext[h, 2 * pair + k, :, pl.ds(first, SPAN)], weights[:, k * BLOCK : (k + 1) * BLOCK])
                attended.append(summed[:HEAD] * (1.0 / summed[HEAD : HEAD + 1]))

        def end():
            rows = jnp.concatenate(attended, axis=0).T.astype(BF16)
            mixed = dot(rows, wso_ref[...])
            hidden = (x_ref[h, pl.ds(first, BLOCK)].astype(F32) + mixed).astype(BF16)
            staged[h, pl.ds(first, BLOCK)] = hidden
            if TURNS[turn]:
                for k in range(2):
                    hidden_copy(2 * b + k, h, ta).start()
            else:
                hidden_copy(partner, h, ta).start()
                mine = pl.ds(pl.multiple_of(ta * part, part), part)
                h_all[ta * hours_dev + h] = staged[h, mine]

        return scores, powers, sums, end

    def spatial_hour(h, carry):
        halo_right(h).wait_recv()
        halo_left(h).wait_recv()
        for side in range(2):
            rows = normed(halo[h, side].astype(F32), gs_ref[...][None])
            keys_values(h, rows, side * (RIM + nodes_dev))
        turns = [spatial_turn(h, turn) for turn in range(blocks_dev)]
        units = [(turn, pair) for turn in turns for pair in range(PAIRS)]
        staggered(units)
        return carry

    lax.fori_loop(0, hours_dev, spatial_hour, 0)

    own_cot.wait()
    others(n_ta, ta, lambda p: cot_copy(p, p).wait_recv())
    for h in range(hours_dev):
        others(n_ta, ta, lambda p, h=h: hidden_copy(p, h, p).wait_recv())

    def split(slab):
        return jnp.concatenate([slab[:, low : low + 8].reshape(BLOCK, WIDTH) for low in (0, 8)], axis=0)

    def joined(rows):
        return jnp.concatenate([rows[low : low + BLOCK].reshape(hours, 8, WIDTH) for low in (0, BLOCK)], axis=1)

    def temporal_group(g, carry):
        nodes = pl.ds(pl.multiple_of(g * GROUP, GROUP), GROUP)
        hidden = split(h_all[:, nodes].astype(F32))
        rows = normed(hidden, gt_ref[...][None])
        keys = dot(rows, wt_ref[:, WIDTH : 2 * WIDTH]).astype(BF16)
        queries = (dot_nt(wt_t[0], rows) * SCORE_SCALE).astype(BF16)
        values = dot_nt(wt_t[1], rows).astype(BF16)
        blank = jnp.zeros((HEAD, BLOCK), BF16)
        ones = jnp.ones((PADDED, BLOCK), BF16)
        attended = []

        def eight_nodes(eight):
            these = slice(eight * BLOCK, (eight + 1) * BLOCK)
            held = {}
            column = []

            def scores(pair):
                heads = slice(pair * BLOCK, (pair + 1) * BLOCK)
                mine = queries[heads, these]
                diagonal = jnp.concatenate(
                    [jnp.concatenate([mine[:HEAD], blank], axis=1), jnp.concatenate([blank, mine[HEAD:]], axis=1)], axis=0
                )
                product = dot(keys[these, heads], diagonal) + bias[...]
                held[pair] = product, jnp.max(fold(product), axis=0, keepdims=True)

            def powers(pair):
                product, largest = held[pair]
                held[pair] = powers_of_two(product - largest)

            def sums(pair):
                weights = held.pop(pair)
                for k in range(2):
                    low = (2 * pair + k) * HEAD
                    summed = dot(
                        jnp.concatenate([values[low : low + HEAD, these], ones], axis=0),
                        weights[:, k * BLOCK : (k + 1) * BLOCK],
                    )
                    column.append(summed[:HEAD] * (1.0 / summed[HEAD : HEAD + 1]))

            def end():
                attended.append(jnp.concatenate(column, axis=0))

            return scores, powers, sums, end

        sets = [eight_nodes(eight) for eight in range(2)]
        staggered([(nodes_set, pair) for nodes_set in sets for pair in range(PAIRS)])
        cot = split(c_all[:, nodes].astype(F32)).astype(BF16)
        g_total[...] += dot(jnp.concatenate(attended, axis=1).astype(BF16), cot)
        mixed = dot(jnp.concatenate([a.T for a in attended], axis=0).astype(BF16), wto_ref[...])
        out_staged[:, nodes] = joined(hidden + mixed).astype(BF16)
        for i in range(1, n_ta):
            out_copy(g, lax.rem(ta + i, n_ta), ta).start()
        return carry

    lax.fori_loop(0, groups, temporal_group, 0)
    own_out = pltpu.make_async_copy(
        out_staged.at[pl.ds(ta * hours_dev, hours_dev)],
        out_ref.at[:, pl.ds(pl.multiple_of(ta * part, part), part)],
        own_sem.at[1],
    )
    own_out.start()

    term = (g_total[...] * tokens ** (-0.5)).astype(BF16)

    def terms_of(core):
        rows = pl.ds(pl.multiple_of(core * owners * PADDED, PADDED), owners * PADDED)
        return dot(picks[rows], term).reshape(owners, PADDED, WIDTH)

    pair_send[...] = terms_of(1 - core).astype(BF16)
    pair_copy.start()
    mine = terms_of(core)
    pair_copy.wait_recv()
    g_send[...] = (mine + pair_recv[...].astype(F32)).astype(BF16)
    to_owners(lambda k: grad_copy(k, core * owners + k, af).start())

    @pl.when(holds)
    def _():
        g_recv[af] = g_send[lax.rem(af, owners)]
        others(n_af, af, lambda p: grad_copy(0, p, p).wait_recv())
        t_send[...] = jnp.sum(g_recv[...].astype(F32), axis=0)
        others(n_ta, ta, lambda p: total_copy(p, ta // 2).start())
        t_recv[ta // 2] = t_send[...]

    def holder_wait(n, carry):
        source = 2 * n + af // owners

        @pl.when(source != ta)
        def _():
            total_copy(source, n).wait_recv()

        return carry

    lax.fori_loop(0, n_ta // 2, holder_wait, 0)
    grad_ref[...] = jnp.sum(t_recv[...], axis=0)[:OWNED]

    def out_waits(g, carry):
        others(n_ta, ta, lambda p: out_copy(g, p, p).wait_recv())
        others(n_ta, ta, lambda p: out_copy(g, p, ta).wait_send())
        return carry

    lax.fori_loop(0, groups, out_waits, 0)
    own_out.wait()
    for h in range(hours_dev):
        halo_right(h).wait_send()
        halo_left(h).wait_send()
        others(n_ta, ta, lambda p, h=h: hidden_copy(p, h, ta).wait_send())
    others(n_ta, ta, lambda p: cot_copy(p, ta).wait_send())
    pair_copy.wait_send()
    to_owners(lambda k: grad_copy(k, core * owners + k, af).wait_send())

    @pl.when(holds)
    def _():
        others(n_ta, ta, lambda p: total_copy(p, ta // 2).wait_send())


def shards(n_ta, n_af, features, ws, wso, wt, wto, gain_s, gain_t, neighbours, degrees, cotangent):
    hours_dev, nodes_dev, width = features.shape
    part = nodes_dev // n_ta
    hours = hours_dev * n_ta
    groups = part // GROUP
    extended = nodes_dev + 2 * RIM
    vmem = pl.BlockSpec(memory_space=pltpu.VMEM)
    anywhere = pl.BlockSpec(memory_space=pl.ANY)
    dma = pltpu.SemaphoreType.DMA
    return pl.pallas_call(
        functools.partial(kernel, n_ta, n_af, hours * nodes_dev * n_af),
        out_shape=(
            jax.ShapeDtypeStruct(features.shape, BF16),
            jax.ShapeDtypeStruct((width // n_af, width), F32),
        ),
        in_specs=[anywhere] * 10,
        out_specs=(anywhere, vmem),
        scratch_shapes=[
            *(pltpu.VMEM(a.shape, a.dtype) for a in (features, ws, wso, wt, wto, gain_s, gain_t)),
            pltpu.SMEM(neighbours.shape, jnp.int32),
            pltpu.SMEM(degrees.shape, jnp.int32),
            pltpu.VMEM((hours_dev, 2, RIM, width), BF16),
            pltpu.VMEM((hours_dev, extended, width), BF16),
            pltpu.VMEM((hours_dev, PAIRS, BLOCK, 2 * nodes_dev), BF16),
            pltpu.VMEM((hours_dev, HEADS, HEAD + PADDED, extended), BF16),
            pltpu.VMEM((2, width, width), BF16),
            pltpu.VMEM((2, width, width), BF16),
            pltpu.VMEM((hours_dev, nodes_dev, width), BF16),
            pltpu.VMEM((hours, part, width), BF16),
            pltpu.VMEM((hours, part, width), BF16),
            pltpu.VMEM((BLOCK, 2 * BLOCK), F32),
            pltpu.VMEM((n_af * PADDED, width), BF16),
            pltpu.VMEM((hours, part, width), BF16),
            pltpu.VMEM((width, width), F32),
            pltpu.VMEM((n_af // 2, PADDED, width), BF16),
            pltpu.VMEM((n_af // 2, PADDED, width), BF16),
            pltpu.VMEM((n_af // 2, PADDED, width), BF16),
            pltpu.VMEM((n_af, PADDED, width), BF16),
            pltpu.VMEM((PADDED, width), F32),
            pltpu.VMEM((n_ta // 2, PADDED, width), F32),
            dma((hours_dev, 2)),
            dma((hours_dev, 2)),
            dma((n_ta,)),
            dma((n_ta,)),
            dma((hours_dev, n_ta)),
            dma((hours_dev, n_ta)),
            dma((groups, n_ta)),
            dma((groups, n_ta)),
            dma((2,)),
            dma((n_af // 2,)),
            dma((n_af,)),
            dma((n_ta,)),
            dma((n_ta // 2,)),
            dma((2,)),
            dma((9,)),
        ],
        compiler_params=pltpu.CompilerParams(
            collective_id=0, has_side_effects=True, vmem_limit_bytes=63 * 2**20
        ),
    )(features, ws, wso, wt, wto, gain_s, gain_t, neighbours, degrees, cotangent)


def solution(mesh):
    return jax.shard_map(
        functools.partial(shards, mesh.shape["ta"], mesh.shape["af"]),
        mesh=mesh,
        in_specs=(
            P("ta", "af", None),
            P(),
            P(),
            P(),
            P(),
            P(),
            P(),
            P("af", None),
            P("af"),
            P("ta", "af", None),
        ),
        out_specs=(P("ta", "af", None), P("af", None)),
        check_vma=False,
    )
```

```python
import functools

import jax
import jax.numpy as jnp
from jax import lax
from jax.experimental import pallas as pl
from jax.experimental.pallas import tpu as pltpu
from jax.sharding import PartitionSpec as P

MESH = pl.DeviceIdType.MESH
F32 = jnp.float32
BF16 = jnp.bfloat16

WIDTH = 384
HEADS = 6
HEAD = 64
PAIRS = 3
BLOCK = 128
RIM = 256
SPAN = 640
WIN = 12
GROUP = 16
OWNED = 12
PADDED = 16
EXCLUDED = 1e30
SCORE_SCALE = 0.125 * 1.4426950408889634


def dot(a, b):
    return jnp.dot(a, b, preferred_element_type=F32)


def dot_nt(a, b):
    return lax.dot_general(a, b, (((1,), (1,)), ((), ())), preferred_element_type=F32)


def normed(rows, gain):
    mean_square = jnp.mean(rows * rows, axis=-1, keepdims=True)
    return (rows * lax.rsqrt(mean_square + 1e-06) * gain).astype(BF16)


def fold(tile):
    widest = tile[:32]
    for low in range(32, tile.shape[0], 32):
        widest = jnp.maximum(widest, tile[low : low + 32])
    widest = jnp.maximum(widest[:16], widest[16:])
    return jnp.maximum(widest[:8], widest[8:])


def powers_of_two(exponents):
    return jnp.exp2(exponents.astype(BF16))


def staggered(units):
    count = len(units)
    for step in range(count + 2):
        if step < count:
            (scores, _, _, _), pair = units[step]
            scores(pair)
        if 0 <= step - 1 < count:
            (_, powers, _, _), pair = units[step - 1]
            powers(pair)
        if 0 <= step - 2:
            (_, _, sums, end), pair = units[step - 2]
            sums(pair)
            if pair == PAIRS - 1:
                end()


def kernel(
    n_ta,
    n_af,
    tokens,
    x_in,
    ws_in,
    wso_in,
    wt_in,
    wto_in,
    gs_in,
    gt_in,
    nb_in,
    dg_in,
    cot_ref,
    out_ref,
    grad_ref,
    x_ref,
    ws_ref,
    wso_ref,
    wt_ref,
    wto_ref,
    gs_ref,
    gt_ref,
    nb_ref,
    dg_ref,
    halo,
    k_ext,
    q_diag,
    v_ext,
    ws_t,
    wt_t,
    staged,
    h_all,
    c_all,
    att,
    bias,
    picks,
    out_staged,
    g_total,
    pair_send,
    pair_recv,
    g_send,
    g_recv,
    t_send,
    t_recv,
    halo_send,
    halo_recv,
    c_send,
    c_recv,
    h_send,
    h_recv,
    o_send,
    o_recv,
    pair_sem,
    gs_sem,
    gr_sem,
    ts_sem,
    tr_sem,
    own_sem,
    in_sem,
):
    ta = lax.axis_index("ta")
    af = lax.axis_index("af")
    hours_dev, nodes_dev, _ = x_in.shape
    part = nodes_dev // n_ta
    blocks_dev = nodes_dev // BLOCK
    hours = hours_dev * n_ta
    groups = part // GROUP
    core = lax.rem(ta, 2)
    partner = ta + 1 - 2 * core
    right = lax.rem(af + 1, n_af)
    left = lax.rem(af + n_af - 1, n_af)

    def to(ta_id, af_id, src, dst, send, recv):
        return pltpu.make_async_remote_copy(
            src_ref=src,
            dst_ref=dst,
            send_sem=send,
            recv_sem=recv,
            device_id=(ta_id, af_id),
            device_id_type=MESH,
        )

    def halo_right(h):
        return to(ta, right, x_in.at[h, pl.ds(nodes_dev - RIM, RIM)], halo.at[h, 0], halo_send.at[h, 0], halo_recv.at[h, 0])

    def halo_left(h):
        return to(ta, left, x_in.at[h, pl.ds(0, RIM)], halo.at[h, 1], halo_send.at[h, 1], halo_recv.at[h, 1])

    def slices(b, peer):
        return pl.ds(pl.multiple_of(b * BLOCK + peer * GROUP, GROUP), GROUP)

    def gathered(b):
        return pl.ds(pl.multiple_of(b * GROUP, GROUP), GROUP)

    def cot_copy(b, peer, slot):
        there = c_all.at[pl.ds(slot * hours_dev, hours_dev), gathered(b)]
        return to(peer, af, cot_ref.at[:, slices(b, peer)], there, c_send.at[b], c_recv.at[b])

    def hidden_copy(b, peer, h, slot):
        there = h_all.at[slot * hours_dev + h, gathered(b)]
        return to(peer, af, staged.at[h, slices(b, peer)], there, h_send.at[b], h_recv.at[b])

    def out_copy(g, peer, slot):
        src = out_staged.at[pl.ds(peer * hours_dev, hours_dev), gathered(g)]
        return to(peer, af, src, out_ref.at[:, slices(g, slot)], o_send.at[g], o_recv.at[g])

    slabs = (pl.ds(0, (n_ta - 1) * hours_dev), pl.ds(0, GROUP))

    def slabs_in(sem):
        to(partner, af, c_all.at[slabs], h_all.at[slabs], own_sem.at[0, 0], sem).wait_recv()

    def slabs_out(sem):
        to(partner, af, c_all.at[slabs], h_all.at[slabs], sem, own_sem.at[0, 0]).wait_send()

    def own_cot(b):
        there = c_all.at[pl.ds(ta * hours_dev, hours_dev), gathered(b)]
        return pltpu.make_async_copy(cot_ref.at[:, slices(b, ta)], there, own_sem.at[0, b])

    def own_out(g):
        src = out_staged.at[pl.ds(ta * hours_dev, hours_dev), gathered(g)]
        return pltpu.make_async_copy(src, out_ref.at[:, slices(g, ta)], own_sem.at[1, g])

    owners = n_af // 2
    holds = af // owners == core
    pair_copy = to(partner, af, pair_send, pair_recv, pair_sem.at[0], pair_sem.at[1])

    def grad_copy(k, owner, slot):
        return to(ta, owner, g_send.at[k], g_recv.at[slot], gs_sem.at[0], gr_sem.at[0])

    def to_owners(act):
        def step(i, carry):
            k = lax.rem(af + i, owners)

            @pl.when(core * owners + k != af)
            def _():
                act(k)

            return carry

        lax.fori_loop(0, owners, step, 0)

    def total_copy(peer, slot):
        return to(peer, af, t_send, t_recv.at[slot], ts_sem.at[0], tr_sem.at[0])

    def others(count, me, act):
        def step(i, carry):
            act(lax.rem(me + i, count))
            return carry

        lax.fori_loop(1, count, step, 0)

    barrier = pltpu.get_barrier_semaphore()
    others(n_ta, ta, lambda p: pl.semaphore_signal(barrier, inc=1, device_id=(p, af), device_id_type=MESH))
    others(n_af, af, lambda p: pl.semaphore_signal(barrier, inc=1, device_id=(ta, p), device_id_type=MESH))

    loads = [
        pltpu.make_async_copy(src, dst, in_sem.at[n])
        for n, (src, dst) in enumerate(
            [
                (ws_in, ws_ref),
                (x_in, x_ref),
                (gs_in, gs_ref),
                (nb_in, nb_ref),
                (dg_in, dg_ref),
                (wso_in, wso_ref),
                (wt_in, wt_ref),
                (wto_in, wto_ref),
                (gt_in, gt_ref),
            ]
        )
    ]
    for load in loads:
        load.start()
    pl.semaphore_wait(barrier, n_ta + n_af - 2)
    halo_right(0).start()
    halo_left(0).start()
    loads[0].wait()
    ws_t[0] = ws_ref[:, :WIDTH].T
    ws_t[1] = ws_ref[:, 2 * WIDTH :].T
    q_diag[...] = jnp.zeros_like(q_diag)
    v_ext[:, :, HEAD:, :] = jnp.ones_like(v_ext[:, :, HEAD:, :])
    for h in range(1, hours_dev):
        halo_right(h).start()
        halo_left(h).start()
    for b in range(blocks_dev):
        others(n_ta, ta, lambda p, b=b: cot_copy(b, p, ta).start())
        own_cot(b).start()

    def keys_values(h, rows_normed, where):
        count = rows_normed.shape[0]
        k_ext[h, pl.ds(where, count), :] = dot(rows_normed, ws_ref[:, WIDTH : 2 * WIDTH]).astype(BF16)
        values = dot_nt(ws_t[1], rows_normed).astype(BF16)
        for head in range(HEADS):
            v_ext[h, head, :HEAD, pl.ds(where, count)] = values[head * HEAD : (head + 1) * HEAD]

    def own_rows(h, carry):
        rows = normed(x_ref[h].astype(F32), gs_ref[...][None])
        keys_values(h, rows, RIM)
        queries = (dot_nt(ws_t[0], rows) * SCORE_SCALE).astype(BF16)
        for pair in range(PAIRS):
            for b in range(blocks_dev):
                for k in range(2):
                    lo = k * (BLOCK // 2)
                    q_diag[h, pair, lo : lo + BLOCK // 2, (2 * b + k) * BLOCK : (2 * b + k + 1) * BLOCK] = queries[
                        pair * BLOCK + lo : pair * BLOCK + lo + BLOCK // 2, b * BLOCK : (b + 1) * BLOCK
                    ]
        return carry

    for load in loads[1:5]:
        load.wait()
    lax.fori_loop(0, hours_dev, own_rows, 0)
    for load in loads[5:]:
        load.wait()

    wt_t[0] = wt_ref[:, :WIDTH].T
    wt_t[1] = wt_ref[:, 2 * WIDTH :].T
    key_index = lax.broadcasted_iota(jnp.int32, bias.shape, 0)
    query_index = lax.broadcasted_iota(jnp.int32, bias.shape, 1) % BLOCK
    ahead = query_index // 8 - key_index // 8
    seen = (query_index % 8 == key_index % 8) & (ahead >= 0) & (ahead < WIN)
    bias[...] = jnp.where(seen, 0.0, -EXCLUDED)
    slot = lax.broadcasted_iota(jnp.int32, picks.shape, 0)
    row = lax.broadcasted_iota(jnp.int32, picks.shape, 1)
    inside = slot % PADDED
    wanted = (inside < OWNED) & (slot // PADDED * OWNED + inside == row)
    picks[...] = jnp.where(wanted, 1.0, 0.0).astype(BF16)
    g_total[...] = jnp.zeros_like(g_total)

    def spatial_turn(h, turn):
        b = turn
        first = b * BLOCK
        penalty = []
        for o in range(5):
            listed = jnp.int32(0)
            for j in range(5):
                hit = (nb_ref[b, j] == af * blocks_dev + b + (o - 2)) & (j < dg_ref[b])
                listed = listed | hit.astype(jnp.int32)
            penalty.append((1 - listed).astype(F32) * EXCLUDED)
        cuts = (((0, 128, 0), (128, 256, 1), (256, 320, 2)), ((0, 64, 2), (64, 192, 3), (192, 320, 4)))
        held = {}
        attended = []

        def scores(pair):
            columns = slice(pair * BLOCK, (pair + 1) * BLOCK)
            queries = q_diag[h, pair, :, pl.ds(b * 2 * BLOCK, 2 * BLOCK)]
            tiles = []
            for part_of, cut in enumerate(cuts):
                start = first + part_of * (SPAN // 2)
                product = dot(k_ext[h, pl.ds(start, SPAN // 2), columns], queries)
                tiles += [(product[low:high], penalty[o]) for low, high, o in cut]
            largest = functools.reduce(jnp.maximum, [fold(tile) - extra for tile, extra in tiles])
            held[pair] = tiles, jnp.max(largest, axis=0, keepdims=True)

        def powers(pair):
            tiles, largest = held[pair]
            held[pair] = jnp.concatenate([powers_of_two(tile - (largest + extra)) for tile, extra in tiles], axis=0)

        def sums(pair):
            weights = held.pop(pair)
            for k in range(2):
                summed = dot(v_ext[h, 2 * pair + k, :, pl.ds(first, SPAN)], weights[:, k * BLOCK : (k + 1) * BLOCK])
                attended.append(summed[:HEAD] * (1.0 / summed[HEAD : HEAD + 1]))

        def end():
            rows = jnp.concatenate(attended, axis=0).T.astype(BF16)
            mixed = dot(rows, wso_ref[...])
            hidden = (x_ref[h, pl.ds(first, BLOCK)].astype(F32) + mixed).astype(BF16)
            staged[h, pl.ds(first, BLOCK)] = hidden
            for i in range(1, n_ta):
                hidden_copy(b, lax.rem(ta + i, n_ta), h, ta).start()
            h_all[ta * hours_dev + h, gathered(b)] = staged[h, slices(b, ta)]

        return scores, powers, sums, end

    def spatial_hour(h, carry):
        halo_right(h).wait_recv()
        halo_left(h).wait_recv()
        for side in range(2):
            rows = normed(halo[h, side].astype(F32), gs_ref[...][None])
            keys_values(h, rows, side * (RIM + nodes_dev))
        turns = [spatial_turn(h, turn) for turn in range(blocks_dev)]
        units = [(turn, pair) for turn in turns for pair in range(PAIRS)]
        staggered(units)
        return carry

    lax.fori_loop(0, hours_dev, spatial_hour, 0)

    def split(slab):
        return jnp.concatenate([slab[:, low : low + 8].reshape(BLOCK, WIDTH) for low in (0, 8)], axis=0)

    def joined(rows):
        return jnp.concatenate([rows[low : low + BLOCK].reshape(hours, 8, WIDTH) for low in (0, BLOCK)], axis=1)

    def temporal_group(g, carry):
        own_cot(g).wait()
        slabs_in(c_recv.at[g])
        slabs_in(h_recv.at[g])
        nodes = gathered(g)
        hidden = split(h_all[:, nodes].astype(F32))
        rows = normed(hidden, gt_ref[...][None])
        keys = dot(rows, wt_ref[:, WIDTH : 2 * WIDTH]).astype(BF16)
        queries = (dot_nt(wt_t[0], rows) * SCORE_SCALE).astype(BF16)
        values = dot_nt(wt_t[1], rows).astype(BF16)
        blank = jnp.zeros((HEAD, BLOCK), BF16)
        ones = jnp.ones((PADDED, BLOCK), BF16)
        attended = []

        def eight_nodes(eight):
            these = slice(eight * BLOCK, (eight + 1) * BLOCK)
            held = {}
            column = []

            def scores(pair):
                heads = slice(pair * BLOCK, (pair + 1) * BLOCK)
                mine = queries[heads, these]
                diagonal = jnp.concatenate(
                    [jnp.concatenate([mine[:HEAD], blank], axis=1), jnp.concatenate([blank, mine[HEAD:]], axis=1)], axis=0
                )
                product = dot(keys[these, heads], diagonal) + bias[...]
                held[pair] = product, jnp.max(fold(product), axis=0, keepdims=True)

            def powers(pair):
                product, largest = held[pair]
                held[pair] = powers_of_two(product - largest)

            def sums(pair):
                weights = held.pop(pair)
                for k in range(2):
                    low = (2 * pair + k) * HEAD
                    summed = dot(
                        jnp.concatenate([values[low : low + HEAD, these], ones], axis=0),
                        weights[:, k * BLOCK : (k + 1) * BLOCK],
                    )
                    column.append(summed[:HEAD] * (1.0 / summed[HEAD : HEAD + 1]))

            def end():
                attended.append(jnp.concatenate(column, axis=0))

            return scores, powers, sums, end

        sets = [eight_nodes(eight) for eight in range(2)]
        staggered([(nodes_set, pair) for nodes_set in sets for pair in range(PAIRS)])
        cot = split(c_all[:, nodes].astype(F32)).astype(BF16)
        g_total[...] += dot(jnp.concatenate(attended, axis=1).astype(BF16), cot)
        att[g] = jnp.concatenate([a.T for a in attended], axis=0).astype(BF16)
        return carry

    def finished(g, carry):
        nodes = gathered(g)
        mixed = dot(att[g], wto_ref[...])
        out_staged[:, nodes] = joined(split(h_all[:, nodes].astype(F32)) + mixed).astype(BF16)
        for i in range(1, n_ta):
            out_copy(g, lax.rem(ta + i, n_ta), ta).start()
        own_out(g).start()
        return carry

    lax.fori_loop(0, groups, temporal_group, 0)

    term = (g_total[...] * tokens ** (-0.5)).astype(BF16)

    def terms_of(core):
        rows = pl.ds(pl.multiple_of(core * owners * PADDED, PADDED), owners * PADDED)
        return dot(picks[rows], term).reshape(owners, PADDED, WIDTH)

    pair_send[...] = terms_of(1 - core).astype(BF16)
    pair_copy.start()
    mine = terms_of(core)
    finished(0, 0)
    pair_copy.wait_recv()
    g_send[...] = (mine + pair_recv[...].astype(F32)).astype(BF16)
    to_owners(lambda k: grad_copy(k, core * owners + k, af).start())
    lax.fori_loop(1, groups, finished, 0)

    def sent(g, carry):
        slabs_out(c_send.at[g])
        slabs_out(h_send.at[g])
        return carry

    lax.fori_loop(0, groups, sent, 0)
    for h in range(hours_dev):
        halo_right(h).wait_send()
        halo_left(h).wait_send()

    def count_waits(held_back, act):
        @pl.when(holds)
        def _():
            act(held_back - 1)

        @pl.when(jnp.logical_not(holds))
        def _():
            act(held_back)

    @pl.when(holds)
    def _():
        g_recv[af] = g_send[lax.rem(af, owners)]
        arrived = g_recv.at[pl.ds(0, n_af - 1)]
        to(partner, af, arrived, arrived, pair_sem.at[0], gr_sem.at[0]).wait_recv()
        t_send[...] = jnp.sum(g_recv[...].astype(F32), axis=0)
        others(n_ta, ta, lambda p: total_copy(p, ta // 2).start())
        t_recv[ta // 2] = t_send[...]

    def out_waits(g, carry):
        slabs_in(o_recv.at[g])
        slabs_out(o_send.at[g])
        own_out(g).wait()
        return carry

    pair_copy.wait_send()

    def terms_sent(count):
        sent_terms = g_send.at[pl.ds(0, count)]
        to(partner, af, sent_terms, sent_terms, gs_sem.at[0], pair_sem.at[1]).wait_send()

    count_waits(owners, terms_sent)
    lax.fori_loop(0, groups, out_waits, 0)

    def totals_in(count):
        totals = t_recv.at[pl.ds(0, count)]
        to(partner, af, totals, totals, pair_sem.at[0], tr_sem.at[0]).wait_recv()

    count_waits(n_ta // 2, totals_in)
    grad_ref[...] = jnp.sum(t_recv[...], axis=0)[:OWNED]

    @pl.when(holds)
    def _():
        sent_rows = g_total.at[pl.ds(0, (n_ta - 1) * PADDED)]
        to(partner, af, sent_rows, sent_rows, ts_sem.at[0], pair_sem.at[1]).wait_send()


def shards(n_ta, n_af, features, ws, wso, wt, wto, gain_s, gain_t, neighbours, degrees, cotangent):
    hours_dev, nodes_dev, width = features.shape
    part = nodes_dev // n_ta
    hours = hours_dev * n_ta
    groups = part // GROUP
    extended = nodes_dev + 2 * RIM
    vmem = pl.BlockSpec(memory_space=pltpu.VMEM)
    anywhere = pl.BlockSpec(memory_space=pl.ANY)
    dma = pltpu.SemaphoreType.DMA
    return pl.pallas_call(
        functools.partial(kernel, n_ta, n_af, hours * nodes_dev * n_af),
        out_shape=(
            jax.ShapeDtypeStruct(features.shape, BF16),
            jax.ShapeDtypeStruct((width // n_af, width), F32),
        ),
        in_specs=[anywhere] * 10,
        out_specs=(anywhere, vmem),
        scratch_shapes=[
            *(pltpu.VMEM(a.shape, a.dtype) for a in (features, ws, wso, wt, wto, gain_s, gain_t)),
            pltpu.SMEM(neighbours.shape, jnp.int32),
            pltpu.SMEM(degrees.shape, jnp.int32),
            pltpu.VMEM((hours_dev, 2, RIM, width), BF16),
            pltpu.VMEM((hours_dev, extended, width), BF16),
            pltpu.VMEM((hours_dev, PAIRS, BLOCK, 2 * nodes_dev), BF16),
            pltpu.VMEM((hours_dev, HEADS, HEAD + PADDED, extended), BF16),
            pltpu.VMEM((2, width, width), BF16),
            pltpu.VMEM((2, width, width), BF16),
            pltpu.VMEM((hours_dev, nodes_dev, width), BF16),
            pltpu.VMEM((hours, part, width), BF16),
            pltpu.VMEM((hours, part, width), BF16),
            pltpu.VMEM((groups, hours * GROUP, width), BF16),
            pltpu.VMEM((BLOCK, 2 * BLOCK), F32),
            pltpu.VMEM((n_af * PADDED, width), BF16),
            pltpu.VMEM((hours, part, width), BF16),
            pltpu.VMEM((width, width), F32),
            pltpu.VMEM((n_af // 2, PADDED, width), BF16),
            pltpu.VMEM((n_af // 2, PADDED, width), BF16),
            pltpu.VMEM((n_af // 2, PADDED, width), BF16),
            pltpu.VMEM((n_af, PADDED, width), BF16),
            pltpu.VMEM((PADDED, width), F32),
            pltpu.VMEM((n_ta // 2, PADDED, width), F32),
            dma((hours_dev, 2)),
            dma((hours_dev, 2)),
            dma((groups,)),
            dma((groups,)),
            dma((groups,)),
            dma((groups,)),
            dma((groups,)),
            dma((groups,)),
            dma((2,)),
            dma((1,)),
            dma((1,)),
            dma((1,)),
            dma((1,)),
            dma((2, groups)),
            dma((9,)),
        ],
        compiler_params=pltpu.CompilerParams(
            collective_id=0, has_side_effects=True, vmem_limit_bytes=63 * 2**20
        ),
    )(features, ws, wso, wt, wto, gain_s, gain_t, neighbours, degrees, cotangent)


def solution(mesh):
    return jax.shard_map(
        functools.partial(shards, mesh.shape["ta"], mesh.shape["af"]),
        mesh=mesh,
        in_specs=(
            P("ta", "af", None),
            P(),
            P(),
            P(),
            P(),
            P(),
            P(),
            P("af", None),
            P("af"),
            P("ta", "af", None),
        ),
        out_specs=(P("ta", "af", None), P("af", None)),
        check_vma=False,
    )
```

```python
import functools

import jax
import jax.numpy as jnp
from jax import lax
from jax.experimental import pallas as pl
from jax.experimental.pallas import tpu as pltpu
from jax.sharding import PartitionSpec as P

MESH = pl.DeviceIdType.MESH
F32 = jnp.float32
BF16 = jnp.bfloat16

WIDTH = 384
HEADS = 6
HEAD = 64
PAIRS = 3
BLOCK = 128
RIM = 256
SPAN = 640
WIN = 12
GROUP = 16
OWNED = 12
PADDED = 16
EXCLUDED = 1e30
SCORE_SCALE = 0.125 * 1.4426950408889634


def dot(a, b):
    return jnp.dot(a, b, preferred_element_type=F32)


def dot_nt(a, b):
    return lax.dot_general(a, b, (((1,), (1,)), ((), ())), preferred_element_type=F32)


def normed(rows, gain):
    mean_square = jnp.mean(rows * rows, axis=-1, keepdims=True)
    return (rows * lax.rsqrt(mean_square + 1e-06) * gain).astype(BF16)


def fold(tile):
    widest = tile[:32]
    for low in range(32, tile.shape[0], 32):
        widest = jnp.maximum(widest, tile[low : low + 32])
    widest = jnp.maximum(widest[:16], widest[16:])
    return jnp.maximum(widest[:8], widest[8:])


def powers_of_two(exponents):
    return jnp.exp2(exponents.astype(BF16))


def staggered(units):
    count = len(units)
    for step in range(count + 2):
        if step < count:
            (scores, _, _, _), pair = units[step]
            scores(pair)
        if 0 <= step - 1 < count:
            (_, powers, _, _), pair = units[step - 1]
            powers(pair)
        if 0 <= step - 2:
            (_, _, sums, end), pair = units[step - 2]
            sums(pair)
            if pair == PAIRS - 1:
                end()


def kernel(
    n_ta,
    n_af,
    tokens,
    x_in,
    ws_in,
    wso_in,
    wt_in,
    wto_in,
    gs_in,
    gt_in,
    nb_in,
    dg_in,
    cot_ref,
    out_ref,
    grad_ref,
    x_ref,
    ws_ref,
    wso_ref,
    wt_ref,
    wto_ref,
    gs_ref,
    gt_ref,
    nb_ref,
    dg_ref,
    halo,
    k_ext,
    q_diag,
    v_ext,
    ws_t,
    wt_t,
    staged,
    h_all,
    c_all,
    att,
    bias,
    picks,
    out_staged,
    g_total,
    pair_send,
    pair_recv,
    g_send,
    g_recv,
    t_send,
    t_recv,
    halo_send,
    halo_recv,
    c_send,
    c_recv,
    h_send,
    h_recv,
    o_send,
    o_recv,
    pair_sem,
    gs_sem,
    gr_sem,
    ts_sem,
    tr_sem,
    own_sem,
    in_sem,
):
    ta = lax.axis_index("ta")
    af = lax.axis_index("af")
    hours_dev, nodes_dev, _ = x_in.shape
    part = nodes_dev // n_ta
    blocks_dev = nodes_dev // BLOCK
    hours = hours_dev * n_ta
    groups = part // GROUP
    core = lax.rem(ta, 2)
    partner = ta + 1 - 2 * core
    right = lax.rem(af + 1, n_af)
    left = lax.rem(af + n_af - 1, n_af)

    def to(ta_id, af_id, src, dst, send, recv):
        return pltpu.make_async_remote_copy(
            src_ref=src,
            dst_ref=dst,
            send_sem=send,
            recv_sem=recv,
            device_id=(ta_id, af_id),
            device_id_type=MESH,
        )

    def halo_right(h):
        return to(ta, right, x_in.at[h, pl.ds(nodes_dev - RIM, RIM)], halo.at[h, 0], halo_send.at[h, 0], halo_recv.at[h, 0])

    def halo_left(h):
        return to(ta, left, x_in.at[h, pl.ds(0, RIM)], halo.at[h, 1], halo_send.at[h, 1], halo_recv.at[h, 1])

    def slices(b, peer):
        return pl.ds(pl.multiple_of(b * BLOCK + peer * GROUP, GROUP), GROUP)

    def gathered(b):
        return pl.ds(pl.multiple_of(b * GROUP, GROUP), GROUP)

    def cot_copy(b, peer, slot):
        there = c_all.at[pl.ds(slot * hours_dev, hours_dev), gathered(b)]
        return to(peer, af, cot_ref.at[:, slices(b, peer)], there, c_send.at[b], c_recv.at[b])

    def hidden_copy(b, peer, h, slot):
        there = h_all.at[slot * hours_dev + h, gathered(b)]
        return to(peer, af, staged.at[h, slices(b, peer)], there, h_send.at[b], h_recv.at[b])

    def out_copy(g, peer, slot):
        src = out_staged.at[pl.ds(peer * hours_dev, hours_dev), gathered(g)]
        return to(peer, af, src, out_ref.at[:, slices(g, slot)], o_send.at[g], o_recv.at[g])

    slabs = (pl.ds(0, (n_ta - 1) * hours_dev), pl.ds(0, GROUP))

    def slabs_in(sem):
        to(partner, af, c_all.at[slabs], h_all.at[slabs], own_sem.at[0, 0], sem).wait_recv()

    def slabs_out(sem):
        to(partner, af, c_all.at[slabs], h_all.at[slabs], sem, own_sem.at[0, 0]).wait_send()

    def own_cot(b):
        there = c_all.at[pl.ds(ta * hours_dev, hours_dev), gathered(b)]
        return pltpu.make_async_copy(cot_ref.at[:, slices(b, ta)], there, own_sem.at[0, b])

    def own_out(g):
        src = out_staged.at[pl.ds(ta * hours_dev, hours_dev), gathered(g)]
        return pltpu.make_async_copy(src, out_ref.at[:, slices(g, ta)], own_sem.at[1, g])

    owners = n_af // 2
    holds = af // owners == core

    def rows_of(core):
        return pl.ds(pl.multiple_of(core * owners * OWNED, GROUP), owners * OWNED)

    pair_copy = to(partner, af, pair_send.at[rows_of(1 - core)], pair_recv, pair_sem.at[0], pair_sem.at[1])

    def grad_copy(k, owner, slot):
        return to(ta, owner, g_send.at[k], g_recv.at[slot], gs_sem.at[0], gr_sem.at[0])

    def to_owners(act):
        def step(i, carry):
            k = lax.rem(af + i, owners)

            @pl.when(core * owners + k != af)
            def _():
                act(k)

            return carry

        lax.fori_loop(0, owners, step, 0)

    def total_copy(peer, slot):
        return to(peer, af, t_send, t_recv.at[slot], ts_sem.at[0], tr_sem.at[0])

    def others(count, me, act):
        def step(i, carry):
            act(lax.rem(me + i, count))
            return carry

        lax.fori_loop(1, count, step, 0)

    barrier = pltpu.get_barrier_semaphore()
    for p in (right, left):
        pl.semaphore_signal(barrier, inc=1, device_id=(ta, p), device_id_type=MESH)

    def greet(i, carry):
        pl.semaphore_signal(barrier, inc=1, device_id=(ta, lax.rem(af + i, n_af)), device_id_type=MESH)
        return carry

    lax.fori_loop(2, n_af - 1, greet, 0)
    others(n_ta, ta, lambda p: pl.semaphore_signal(barrier, inc=1, device_id=(p, af), device_id_type=MESH))

    loads = [
        pltpu.make_async_copy(src, dst, in_sem.at[n])
        for n, (src, dst) in enumerate(
            [
                (ws_in, ws_ref),
                (x_in, x_ref),
                (gs_in, gs_ref),
                (nb_in, nb_ref),
                (dg_in, dg_ref),
                (wso_in, wso_ref),
                (wt_in, wt_ref),
                (wto_in, wto_ref),
                (gt_in, gt_ref),
            ]
        )
    ]
    for load in loads:
        load.start()
    pl.semaphore_wait(barrier, n_ta + n_af - 2)
    halo_right(0).start()
    halo_left(0).start()
    loads[0].wait()
    ws_t[0] = ws_ref[:, :WIDTH].T
    ws_t[1] = ws_ref[:, 2 * WIDTH :].T
    q_diag[...] = jnp.zeros_like(q_diag)
    v_ext[:, :, HEAD:, :] = jnp.ones_like(v_ext[:, :, HEAD:, :])
    for h in range(1, hours_dev):
        halo_right(h).start()
        halo_left(h).start()
    for b in range(blocks_dev):
        others(n_ta, ta, lambda p, b=b: cot_copy(b, p, ta).start())
        own_cot(b).start()

    def keys_values(h, rows_normed, where):
        count = rows_normed.shape[0]
        k_ext[h, pl.ds(where, count), :] = dot(rows_normed, ws_ref[:, WIDTH : 2 * WIDTH]).astype(BF16)
        values = dot_nt(ws_t[1], rows_normed).astype(BF16)
        for head in range(HEADS):
            v_ext[h, head, :HEAD, pl.ds(where, count)] = values[head * HEAD : (head + 1) * HEAD]

    def own_rows(h, carry):
        rows = normed(x_ref[h].astype(F32), gs_ref[...][None])
        keys_values(h, rows, RIM)
        queries = (dot_nt(ws_t[0], rows) * SCORE_SCALE).astype(BF16)
        for pair in range(PAIRS):
            for b in range(blocks_dev):
                for k in range(2):
                    lo = k * (BLOCK // 2)
                    q_diag[h, pair, lo : lo + BLOCK // 2, (2 * b + k) * BLOCK : (2 * b + k + 1) * BLOCK] = queries[
                        pair * BLOCK + lo : pair * BLOCK + lo + BLOCK // 2, b * BLOCK : (b + 1) * BLOCK
                    ]
        return carry

    for load in loads[1:5]:
        load.wait()
    lax.fori_loop(0, hours_dev, own_rows, 0)
    for load in loads[5:]:
        load.wait()

    wt_t[0] = wt_ref[:, :WIDTH].T
    wt_t[1] = wt_ref[:, 2 * WIDTH :].T
    key_index = lax.broadcasted_iota(jnp.int32, bias.shape, 0)
    query_index = lax.broadcasted_iota(jnp.int32, bias.shape, 1) % BLOCK
    ahead = query_index // 8 - key_index // 8
    seen = (query_index % 8 == key_index % 8) & (ahead >= 0) & (ahead < WIN)
    bias[...] = jnp.where(seen, 0.0, -EXCLUDED)
    slot = lax.broadcasted_iota(jnp.int32, picks.shape, 0)
    row = lax.broadcasted_iota(jnp.int32, picks.shape, 1)
    inside = slot % PADDED
    wanted = (inside < OWNED) & (slot // PADDED * OWNED + inside == row)
    picks[...] = jnp.where(wanted, 1.0, 0.0).astype(BF16)
    g_total[...] = jnp.zeros_like(g_total)

    def spatial_turn(h, turn):
        b = turn
        first = b * BLOCK
        penalty = []
        for o in range(5):
            listed = jnp.int32(0)
            for j in range(5):
                hit = (nb_ref[b, j] == af * blocks_dev + b + (o - 2)) & (j < dg_ref[b])
                listed = listed | hit.astype(jnp.int32)
            penalty.append((1 - listed).astype(F32) * EXCLUDED)
        cuts = (((0, 128, 0), (128, 256, 1), (256, 320, 2)), ((0, 64, 2), (64, 192, 3), (192, 320, 4)))
        held = {}
        attended = []

        def scores(pair):
            columns = slice(pair * BLOCK, (pair + 1) * BLOCK)
            queries = q_diag[h, pair, :, pl.ds(b * 2 * BLOCK, 2 * BLOCK)]
            tiles = []
            for part_of, cut in enumerate(cuts):
                start = first + part_of * (SPAN // 2)
                product = dot(k_ext[h, pl.ds(start, SPAN // 2), columns], queries)
                tiles += [(product[low:high], penalty[o]) for low, high, o in cut]
            largest = functools.reduce(jnp.maximum, [fold(tile) - extra for tile, extra in tiles])
            held[pair] = tiles, jnp.max(largest, axis=0, keepdims=True)

        def powers(pair):
            tiles, largest = held[pair]
            held[pair] = jnp.concatenate([powers_of_two(tile - (largest + extra)) for tile, extra in tiles], axis=0)

        def sums(pair):
            weights = held.pop(pair)
            for k in range(2):
                summed = dot(v_ext[h, 2 * pair + k, :, pl.ds(first, SPAN)], weights[:, k * BLOCK : (k + 1) * BLOCK])
                attended.append(summed[:HEAD] * (1.0 / summed[HEAD : HEAD + 1]))

        def end():
            rows = jnp.concatenate(attended, axis=0).T.astype(BF16)
            mixed = dot(rows, wso_ref[...])
            hidden = (x_ref[h, pl.ds(first, BLOCK)].astype(F32) + mixed).astype(BF16)
            staged[h, pl.ds(first, BLOCK)] = hidden
            for i in range(1, n_ta):
                hidden_copy(b, lax.rem(ta + i, n_ta), h, ta).start()
            h_all[ta * hours_dev + h, gathered(b)] = staged[h, slices(b, ta)]

        return scores, powers, sums, end

    def spatial_hour(h, carry):
        halo_right(h).wait_recv()
        halo_left(h).wait_recv()
        for side in range(2):
            rows = normed(halo[h, side].astype(F32), gs_ref[...][None])
            keys_values(h, rows, side * (RIM + nodes_dev))
        turns = [spatial_turn(h, turn) for turn in range(blocks_dev)]
        units = [(turn, pair) for turn in turns for pair in range(PAIRS)]
        staggered(units)
        return carry

    lax.fori_loop(0, hours_dev, spatial_hour, 0)

    def split(slab):
        return jnp.concatenate([slab[:, low : low + 8].reshape(BLOCK, WIDTH) for low in (0, 8)], axis=0)

    def joined(rows):
        return jnp.concatenate([rows[low : low + BLOCK].reshape(hours, 8, WIDTH) for low in (0, BLOCK)], axis=1)

    def temporal_group(g, carry):
        own_cot(g).wait()
        slabs_in(c_recv.at[g])
        slabs_in(h_recv.at[g])
        nodes = gathered(g)
        hidden = split(h_all[:, nodes].astype(F32))
        rows = normed(hidden, gt_ref[...][None])
        keys = dot(rows, wt_ref[:, WIDTH : 2 * WIDTH]).astype(BF16)
        queries = (dot_nt(wt_t[0], rows) * SCORE_SCALE).astype(BF16)
        values = dot_nt(wt_t[1], rows).astype(BF16)
        blank = jnp.zeros((HEAD, BLOCK), BF16)
        ones = jnp.ones((PADDED, BLOCK), BF16)
        attended = []

        def eight_nodes(eight):
            these = slice(eight * BLOCK, (eight + 1) * BLOCK)
            held = {}
            column = []

            def scores(pair):
                heads = slice(pair * BLOCK, (pair + 1) * BLOCK)
                mine = queries[heads, these]
                diagonal = jnp.concatenate(
                    [jnp.concatenate([mine[:HEAD], blank], axis=1), jnp.concatenate([blank, mine[HEAD:]], axis=1)], axis=0
                )
                product = dot(keys[these, heads], diagonal) + bias[...]
                held[pair] = product, jnp.max(fold(product), axis=0, keepdims=True)

            def powers(pair):
                product, largest = held[pair]
                held[pair] = powers_of_two(product - largest)

            def sums(pair):
                weights = held.pop(pair)
                for k in range(2):
                    low = (2 * pair + k) * HEAD
                    summed = dot(
                        jnp.concatenate([values[low : low + HEAD, these], ones], axis=0),
                        weights[:, k * BLOCK : (k + 1) * BLOCK],
                    )
                    column.append(summed[:HEAD] * (1.0 / summed[HEAD : HEAD + 1]))

            def end():
                attended.append(jnp.concatenate(column, axis=0))

            return scores, powers, sums, end

        sets = [eight_nodes(eight) for eight in range(2)]
        staggered([(nodes_set, pair) for nodes_set in sets for pair in range(PAIRS)])
        cot = split(c_all[:, nodes].astype(F32)).astype(BF16)
        g_total[...] += dot(jnp.concatenate(attended, axis=1).astype(BF16), cot)
        att[g] = jnp.concatenate([a.T for a in attended], axis=0).astype(BF16)
        return carry

    def finished(g, carry):
        nodes = gathered(g)
        mixed = dot(att[g], wto_ref[...])
        out_staged[:, nodes] = joined(split(h_all[:, nodes].astype(F32)) + mixed).astype(BF16)
        for i in range(1, n_ta):
            out_copy(g, lax.rem(ta + i, n_ta), ta).start()
        own_out(g).start()
        return carry

    lax.fori_loop(0, groups, temporal_group, 0)

    pair_send[...] = (g_total[...] * tokens ** (-0.5)).astype(BF16)
    pair_copy.start()
    finished(0, 0)
    pair_copy.wait_recv()
    both = (pair_send[rows_of(core)].astype(F32) + pair_recv[...].astype(F32)).astype(BF16)
    g_send[...] = dot(picks[...], both).astype(BF16).reshape(owners, PADDED, WIDTH)
    to_owners(lambda k: grad_copy(k, core * owners + k, af).start())
    lax.fori_loop(1, groups, finished, 0)

    def sent(g, carry):
        slabs_out(c_send.at[g])
        slabs_out(h_send.at[g])
        return carry

    lax.fori_loop(0, groups, sent, 0)
    for h in range(hours_dev):
        halo_right(h).wait_send()
        halo_left(h).wait_send()

    def count_waits(held_back, act):
        @pl.when(holds)
        def _():
            act(held_back - 1)

        @pl.when(jnp.logical_not(holds))
        def _():
            act(held_back)

    @pl.when(holds)
    def _():
        g_recv[af] = g_send[lax.rem(af, owners)]
        arrived = g_recv.at[pl.ds(0, n_af - 1)]
        to(partner, af, arrived, arrived, pair_sem.at[0], gr_sem.at[0]).wait_recv()
        t_send[...] = jnp.sum(g_recv[...].astype(F32), axis=0)
        others(n_ta, ta, lambda p: total_copy(p, ta // 2).start())
        t_recv[ta // 2] = t_send[...]

    def out_waits(g, carry):
        slabs_in(o_recv.at[g])
        slabs_out(o_send.at[g])
        own_out(g).wait()
        return carry

    pair_copy.wait_send()

    def terms_sent(count):
        sent_terms = g_send.at[pl.ds(0, count)]
        to(partner, af, sent_terms, sent_terms, gs_sem.at[0], pair_sem.at[1]).wait_send()

    count_waits(owners, terms_sent)
    lax.fori_loop(0, groups, out_waits, 0)

    def totals_in(count):
        totals = t_recv.at[pl.ds(0, count)]
        to(partner, af, totals, totals, pair_sem.at[0], tr_sem.at[0]).wait_recv()

    count_waits(n_ta // 2, totals_in)
    grad_ref[...] = jnp.sum(t_recv[...], axis=0)[:OWNED]

    @pl.when(holds)
    def _():
        sent_rows = g_total.at[pl.ds(0, (n_ta - 1) * PADDED)]
        to(partner, af, sent_rows, sent_rows, ts_sem.at[0], pair_sem.at[1]).wait_send()


def shards(n_ta, n_af, features, ws, wso, wt, wto, gain_s, gain_t, neighbours, degrees, cotangent):
    hours_dev, nodes_dev, width = features.shape
    part = nodes_dev // n_ta
    hours = hours_dev * n_ta
    groups = part // GROUP
    extended = nodes_dev + 2 * RIM
    vmem = pl.BlockSpec(memory_space=pltpu.VMEM)
    anywhere = pl.BlockSpec(memory_space=pl.ANY)
    dma = pltpu.SemaphoreType.DMA
    return pl.pallas_call(
        functools.partial(kernel, n_ta, n_af, hours * nodes_dev * n_af),
        out_shape=(
            jax.ShapeDtypeStruct(features.shape, BF16),
            jax.ShapeDtypeStruct((width // n_af, width), F32),
        ),
        in_specs=[anywhere] * 10,
        out_specs=(anywhere, vmem),
        scratch_shapes=[
            *(pltpu.VMEM(a.shape, a.dtype) for a in (features, ws, wso, wt, wto, gain_s, gain_t)),
            pltpu.SMEM(neighbours.shape, jnp.int32),
            pltpu.SMEM(degrees.shape, jnp.int32),
            pltpu.VMEM((hours_dev, 2, RIM, width), BF16),
            pltpu.VMEM((hours_dev, extended, width), BF16),
            pltpu.VMEM((hours_dev, PAIRS, BLOCK, 2 * nodes_dev), BF16),
            pltpu.VMEM((hours_dev, HEADS, HEAD + PADDED, extended), BF16),
            pltpu.VMEM((2, width, width), BF16),
            pltpu.VMEM((2, width, width), BF16),
            pltpu.VMEM((hours_dev, nodes_dev, width), BF16),
            pltpu.VMEM((hours, part, width), BF16),
            pltpu.VMEM((hours, part, width), BF16),
            pltpu.VMEM((groups, hours * GROUP, width), BF16),
            pltpu.VMEM((BLOCK, 2 * BLOCK), F32),
            pltpu.VMEM((n_af // 2 * PADDED, n_af // 2 * OWNED), BF16),
            pltpu.VMEM((hours, part, width), BF16),
            pltpu.VMEM((width, width), F32),
            pltpu.VMEM((width, width), BF16),
            pltpu.VMEM((width // 2, width), BF16),
            pltpu.VMEM((n_af // 2, PADDED, width), BF16),
            pltpu.VMEM((n_af, PADDED, width), BF16),
            pltpu.VMEM((PADDED, width), F32),
            pltpu.VMEM((n_ta // 2, PADDED, width), F32),
            dma((hours_dev, 2)),
            dma((hours_dev, 2)),
            dma((groups,)),
            dma((groups,)),
            dma((groups,)),
            dma((groups,)),
            dma((groups,)),
            dma((groups,)),
            dma((2,)),
            dma((1,)),
            dma((1,)),
            dma((1,)),
            dma((1,)),
            dma((2, groups)),
            dma((9,)),
        ],
        compiler_params=pltpu.CompilerParams(
            collective_id=0, has_side_effects=True, vmem_limit_bytes=63 * 2**20
        ),
    )(features, ws, wso, wt, wto, gain_s, gain_t, neighbours, degrees, cotangent)


def solution(mesh):
    return jax.shard_map(
        functools.partial(shards, mesh.shape["ta"], mesh.shape["af"]),
        mesh=mesh,
        in_specs=(
            P("ta", "af", None),
            P(),
            P(),
            P(),
            P(),
            P(),
            P(),
            P("af", None),
            P("af"),
            P("ta", "af", None),
        ),
        out_specs=(P("ta", "af", None), P("af", None)),
        check_vma=False,
    )
```

```python
import functools

import jax
import jax.numpy as jnp
from jax import lax
from jax.experimental import pallas as pl
from jax.experimental.pallas import tpu as pltpu
from jax.sharding import PartitionSpec as P

MESH = pl.DeviceIdType.MESH
F32 = jnp.float32
BF16 = jnp.bfloat16

WIDTH = 384
HEADS = 6
HEAD = 64
PAIRS = 3
BLOCK = 128
RIM = 256
SPAN = 640
WIN = 12
GROUP = 16
OWNED = 12
PADDED = 16
EXCLUDED = 1e30
SCORE_SCALE = 0.125 * 1.4426950408889634


def dot(a, b):
    return jnp.dot(a, b, preferred_element_type=F32)


def dot_nt(a, b):
    return lax.dot_general(a, b, (((1,), (1,)), ((), ())), preferred_element_type=F32)


def normed(rows, gain):
    mean_square = jnp.mean(rows * rows, axis=-1, keepdims=True)
    return (rows * lax.rsqrt(mean_square + 1e-06) * gain).astype(BF16)


def fold(tile):
    widest = tile[:32]
    for low in range(32, tile.shape[0], 32):
        widest = jnp.maximum(widest, tile[low : low + 32])
    widest = jnp.maximum(widest[:16], widest[16:])
    return jnp.maximum(widest[:8], widest[8:])


def powers_of_two(exponents):
    return jnp.exp2(exponents.astype(BF16))


def staggered(units):
    count = len(units)
    for step in range(count + 2):
        if step < count:
            (scores, _, _, _), pair = units[step]
            scores(pair)
        if 0 <= step - 1 < count:
            (_, powers, _, _), pair = units[step - 1]
            powers(pair)
        if 0 <= step - 2:
            (_, _, sums, end), pair = units[step - 2]
            sums(pair)
            if pair == PAIRS - 1:
                end()


def kernel(
    n_ta,
    n_af,
    tokens,
    x_in,
    ws_in,
    wso_in,
    wt_in,
    wto_in,
    gs_in,
    gt_in,
    nb_in,
    dg_in,
    cot_ref,
    out_ref,
    grad_ref,
    x_ref,
    ws_ref,
    wso_ref,
    wt_ref,
    wto_ref,
    gs_ref,
    gt_ref,
    nb_ref,
    dg_ref,
    halo,
    k_ext,
    q_diag,
    v_ext,
    ws_t,
    wt_t,
    staged,
    h_all,
    c_all,
    att,
    bias,
    picks,
    out_staged,
    g_total,
    pair_send,
    pair_recv,
    g_send,
    g_recv,
    t_send,
    t_recv,
    halo_send,
    halo_recv,
    c_send,
    c_recv,
    h_send,
    h_recv,
    o_send,
    o_recv,
    pair_sem,
    gs_sem,
    gr_sem,
    ts_sem,
    tr_sem,
    own_sem,
    in_sem,
):
    ta = lax.axis_index("ta")
    af = lax.axis_index("af")
    hours_dev, nodes_dev, _ = x_in.shape
    part = nodes_dev // n_ta
    blocks_dev = nodes_dev // BLOCK
    hours = hours_dev * n_ta
    groups = part // GROUP
    core = lax.rem(ta, 2)
    partner = ta + 1 - 2 * core
    right = lax.rem(af + 1, n_af)
    left = lax.rem(af + n_af - 1, n_af)

    def to(ta_id, af_id, src, dst, send, recv):
        return pltpu.make_async_remote_copy(
            src_ref=src,
            dst_ref=dst,
            send_sem=send,
            recv_sem=recv,
            device_id=(ta_id, af_id),
            device_id_type=MESH,
        )

    def halo_right(h):
        return to(ta, right, x_in.at[h, pl.ds(nodes_dev - RIM, RIM)], halo.at[h, 0], halo_send.at[h, 0], halo_recv.at[h, 0])

    def halo_left(h):
        return to(ta, left, x_in.at[h, pl.ds(0, RIM)], halo.at[h, 1], halo_send.at[h, 1], halo_recv.at[h, 1])

    def slices(b, peer):
        return pl.ds(pl.multiple_of(b * BLOCK + peer * GROUP, GROUP), GROUP)

    def gathered(b):
        return pl.ds(pl.multiple_of(b * GROUP, GROUP), GROUP)

    def cot_copy(b, peer, slot):
        there = c_all.at[pl.ds(slot * hours_dev, hours_dev), gathered(b)]
        return to(peer, af, cot_ref.at[:, slices(b, peer)], there, c_send.at[b], c_recv.at[b])

    def hidden_copy(two, peer, h, slot):
        pair_of = pl.ds(2 * two, 2)
        rows = pl.ds(pl.multiple_of(peer * GROUP, GROUP), GROUP)
        there = h_all.at[slot * hours_dev + h, pair_of]
        return to(peer, af, staged.at[h, pair_of, rows], there, h_send.at[two], h_recv.at[two])

    def out_copy(g, peer, slot):
        src = out_staged.at[pl.ds(peer * hours_dev, hours_dev), gathered(g)]
        return to(peer, af, src, out_ref.at[:, slices(g, slot)], o_send.at[g], o_recv.at[g])

    slabs = (pl.ds(0, (n_ta - 1) * hours_dev), pl.ds(0, GROUP))

    def slabs_in(sem):
        to(partner, af, c_all.at[slabs], out_staged.at[slabs], own_sem.at[0, 0], sem).wait_recv()

    twos = (pl.ds(0, (n_ta - 1) * hours_dev), pl.ds(0, 2))

    def slabs_out(sem):
        to(partner, af, c_all.at[slabs], out_staged.at[slabs], sem, own_sem.at[0, 0]).wait_send()

    def own_cot(b):
        there = c_all.at[pl.ds(ta * hours_dev, hours_dev), gathered(b)]
        return pltpu.make_async_copy(cot_ref.at[:, slices(b, ta)], there, own_sem.at[0, b])

    def own_out(g):
        src = out_staged.at[pl.ds(ta * hours_dev, hours_dev), gathered(g)]
        return pltpu.make_async_copy(src, out_ref.at[:, slices(g, ta)], own_sem.at[1, g])

    owners = n_af // 2
    holds = af // owners == core

    def rows_of(core):
        return pl.ds(pl.multiple_of(core * owners * OWNED, GROUP), owners * OWNED)

    pair_copy = to(partner, af, pair_send.at[rows_of(1 - core)], pair_recv, pair_sem.at[0], pair_sem.at[1])

    def grad_copy(k, owner, slot):
        return to(ta, owner, g_send.at[k], g_recv.at[slot], gs_sem.at[0], gr_sem.at[0])

    def to_owners(act):
        def step(i, carry):
            k = lax.rem(af + i, owners)

            @pl.when(core * owners + k != af)
            def _():
                act(k)

            return carry

        lax.fori_loop(0, owners, step, 0)

    def total_copy(peer, slot):
        return to(peer, af, t_send, t_recv.at[slot], ts_sem.at[0], tr_sem.at[0])

    def others(count, me, act):
        def step(i, carry):
            act(lax.rem(me + i, count))
            return carry

        lax.fori_loop(1, count, step, 0)

    barrier = pltpu.get_barrier_semaphore()
    for p in (right, left):
        pl.semaphore_signal(barrier, inc=1, device_id=(ta, p), device_id_type=MESH)

    def greet(i, carry):
        pl.semaphore_signal(barrier, inc=1, device_id=(ta, lax.rem(af + i, n_af)), device_id_type=MESH)
        return carry

    lax.fori_loop(2, n_af - 1, greet, 0)
    others(n_ta, ta, lambda p: pl.semaphore_signal(barrier, inc=1, device_id=(p, af), device_id_type=MESH))

    loads = [
        pltpu.make_async_copy(src, dst, in_sem.at[n])
        for n, (src, dst) in enumerate(
            [
                (ws_in, ws_ref),
                (x_in, x_ref),
                (gs_in, gs_ref),
                (nb_in, nb_ref),
                (dg_in, dg_ref),
                (wso_in, wso_ref),
                (wt_in, wt_ref),
                (wto_in, wto_ref),
                (gt_in, gt_ref),
            ]
        )
    ]
    for load in loads:
        load.start()
    pl.semaphore_wait(barrier, n_ta + n_af - 2)
    halo_right(0).start()
    halo_left(0).start()
    loads[0].wait()
    ws_t[0] = ws_ref[:, :WIDTH].T
    ws_t[1] = ws_ref[:, 2 * WIDTH :].T
    q_diag[...] = jnp.zeros_like(q_diag)
    v_ext[:, :, HEAD:, :] = jnp.ones_like(v_ext[:, :, HEAD:, :])
    for h in range(1, hours_dev):
        halo_right(h).start()
        halo_left(h).start()
    for b in range(blocks_dev):
        others(n_ta, ta, lambda p, b=b: cot_copy(b, p, ta).start())
        own_cot(b).start()

    def keys_values(h, rows_normed, where):
        count = rows_normed.shape[0]
        k_ext[h, pl.ds(where, count), :] = dot(rows_normed, ws_ref[:, WIDTH : 2 * WIDTH]).astype(BF16)
        values = dot_nt(ws_t[1], rows_normed).astype(BF16)
        for head in range(HEADS):
            v_ext[h, head, :HEAD, pl.ds(where, count)] = values[head * HEAD : (head + 1) * HEAD]

    def own_rows(h, carry):
        rows = normed(x_ref[h].astype(F32), gs_ref[...][None])
        keys_values(h, rows, RIM)
        queries = (dot_nt(ws_t[0], rows) * SCORE_SCALE).astype(BF16)
        for pair in range(PAIRS):
            for b in range(blocks_dev):
                for k in range(2):
                    lo = k * (BLOCK // 2)
                    q_diag[h, pair, lo : lo + BLOCK // 2, (2 * b + k) * BLOCK : (2 * b + k + 1) * BLOCK] = queries[
                        pair * BLOCK + lo : pair * BLOCK + lo + BLOCK // 2, b * BLOCK : (b + 1) * BLOCK
                    ]
        return carry

    for load in loads[1:5]:
        load.wait()
    lax.fori_loop(0, hours_dev, own_rows, 0)
    for load in loads[5:]:
        load.wait()

    wt_t[0] = wt_ref[:, :WIDTH].T
    wt_t[1] = wt_ref[:, 2 * WIDTH :].T
    key_index = lax.broadcasted_iota(jnp.int32, bias.shape, 0)
    query_index = lax.broadcasted_iota(jnp.int32, bias.shape, 1) % BLOCK
    ahead = query_index // 8 - key_index // 8
    seen = (query_index % 8 == key_index % 8) & (ahead >= 0) & (ahead < WIN)
    bias[...] = jnp.where(seen, 0.0, -EXCLUDED)
    slot = lax.broadcasted_iota(jnp.int32, picks.shape, 0)
    row = lax.broadcasted_iota(jnp.int32, picks.shape, 1)
    inside = slot % PADDED
    wanted = (inside < OWNED) & (slot // PADDED * OWNED + inside == row)
    picks[...] = jnp.where(wanted, 1.0, 0.0).astype(BF16)
    g_total[...] = jnp.zeros_like(g_total)

    def spatial_turn(h, turn):
        b = turn
        first = b * BLOCK
        penalty = []
        for o in range(5):
            listed = jnp.int32(0)
            for j in range(5):
                hit = (nb_ref[b, j] == af * blocks_dev + b + (o - 2)) & (j < dg_ref[b])
                listed = listed | hit.astype(jnp.int32)
            penalty.append((1 - listed).astype(F32) * EXCLUDED)
        cuts = (((0, 128, 0), (128, 256, 1), (256, 320, 2)), ((0, 64, 2), (64, 192, 3), (192, 320, 4)))
        held = {}
        attended = []

        def scores(pair):
            columns = slice(pair * BLOCK, (pair + 1) * BLOCK)
            queries = q_diag[h, pair, :, pl.ds(b * 2 * BLOCK, 2 * BLOCK)]
            tiles = []
            for part_of, cut in enumerate(cuts):
                start = first + part_of * (SPAN // 2)
                product = dot(k_ext[h, pl.ds(start, SPAN // 2), columns], queries)
                tiles += [(product[low:high], penalty[o]) for low, high, o in cut]
            largest = functools.reduce(jnp.maximum, [fold(tile) - extra for tile, extra in tiles])
            held[pair] = tiles, jnp.max(largest, axis=0, keepdims=True)

        def powers(pair):
            tiles, largest = held[pair]
            held[pair] = jnp.concatenate([powers_of_two(tile - (largest + extra)) for tile, extra in tiles], axis=0)

        def sums(pair):
            weights = held.pop(pair)
            for k in range(2):
                summed = dot(v_ext[h, 2 * pair + k, :, pl.ds(first, SPAN)], weights[:, k * BLOCK : (k + 1) * BLOCK])
                attended.append(summed[:HEAD] * (1.0 / summed[HEAD : HEAD + 1]))

        def end():
            rows = jnp.concatenate(attended, axis=0).T.astype(BF16)
            mixed = dot(rows, wso_ref[...])
            hidden = (x_ref[h, pl.ds(first, BLOCK)].astype(F32) + mixed).astype(BF16)
            staged[h, b] = hidden
            h_all[ta * hours_dev + h, b] = staged[h, b, pl.ds(pl.multiple_of(ta * GROUP, GROUP), GROUP)]
            if b % 2:
                for i in range(1, n_ta):
                    hidden_copy(b // 2, lax.rem(ta + i, n_ta), h, ta).start()

        return scores, powers, sums, end

    def spatial_hour(h, carry):
        halo_right(h).wait_recv()
        halo_left(h).wait_recv()
        for side in range(2):
            rows = normed(halo[h, side].astype(F32), gs_ref[...][None])
            keys_values(h, rows, side * (RIM + nodes_dev))
        turns = [spatial_turn(h, turn) for turn in range(blocks_dev)]
        units = [(turn, pair) for turn in turns for pair in range(PAIRS)]
        staggered(units)
        return carry

    lax.fori_loop(0, hours_dev, spatial_hour, 0)

    def split(slab):
        return jnp.concatenate([slab[:, low : low + 8].reshape(BLOCK, WIDTH) for low in (0, 8)], axis=0)

    def joined(rows):
        return jnp.concatenate([rows[low : low + BLOCK].reshape(hours, 8, WIDTH) for low in (0, BLOCK)], axis=1)

    def group_parts(g):
        hidden = split(h_all[:, g].astype(F32))
        rows = normed(hidden, gt_ref[...][None])
        keys = dot(rows, wt_ref[:, WIDTH : 2 * WIDTH]).astype(BF16)
        queries = (dot_nt(wt_t[0], rows) * SCORE_SCALE).astype(BF16)
        values = dot_nt(wt_t[1], rows).astype(BF16)
        blank = jnp.zeros((HEAD, BLOCK), BF16)
        ones = jnp.ones((PADDED, BLOCK), BF16)
        attended = []

        def eight_nodes(eight):
            these = slice(eight * BLOCK, (eight + 1) * BLOCK)
            held = {}
            column = []

            def scores(pair):
                heads = slice(pair * BLOCK, (pair + 1) * BLOCK)
                mine = queries[heads, these]
                diagonal = jnp.concatenate(
                    [jnp.concatenate([mine[:HEAD], blank], axis=1), jnp.concatenate([blank, mine[HEAD:]], axis=1)], axis=0
                )
                product = dot(keys[these, heads], diagonal) + bias[...]
                held[pair] = product, jnp.max(fold(product), axis=0, keepdims=True)

            def powers(pair):
                product, largest = held[pair]
                held[pair] = powers_of_two(product - largest)

            def sums(pair):
                weights = held.pop(pair)
                for k in range(2):
                    low = (2 * pair + k) * HEAD
                    summed = dot(
                        jnp.concatenate([values[low : low + HEAD, these], ones], axis=0),
                        weights[:, k * BLOCK : (k + 1) * BLOCK],
                    )
                    column.append(summed[:HEAD] * (1.0 / summed[HEAD : HEAD + 1]))

            def end():
                attended.append(jnp.concatenate(column, axis=0))
                if eight:
                    att[g] = jnp.concatenate([a.T for a in attended], axis=0).astype(BF16)

            return scores, powers, sums, end

        return attended, [eight_nodes(eight) for eight in range(2)]

    def temporal_two(two, carry):
        to(partner, af, h_all.at[twos], h_all.at[twos], own_sem.at[0, 0], h_recv.at[two]).wait_recv()
        cots = []
        parts = []
        for k in range(2):
            g = 2 * two + k
            own_cot(g).wait()
            slabs_in(c_recv.at[g])
            parts.append(group_parts(g))
        staggered([(steps, pair) for _, sets in parts for steps in sets for pair in range(PAIRS)])
        for k in range(2):
            cots.append(split(c_all[:, gathered(2 * two + k)].astype(F32)).astype(BF16))
        everything = jnp.concatenate([a for attended, _ in parts for a in attended], axis=1).astype(BF16)
        g_total[...] += dot(everything, jnp.concatenate(cots, axis=0))
        return carry

    def finished(g, carry):
        nodes = gathered(g)
        mixed = dot(att[g], wto_ref[...])
        out_staged[:, nodes] = joined(split(h_all[:, g].astype(F32)) + mixed).astype(BF16)
        for i in range(1, n_ta):
            out_copy(g, lax.rem(ta + i, n_ta), ta).start()
        own_out(g).start()
        return carry

    lax.fori_loop(0, groups // 2, temporal_two, 0)

    pair_send[...] = (g_total[...] * tokens ** (-0.5)).astype(BF16)
    pair_copy.start()
    finished(0, 0)
    pair_copy.wait_recv()
    both = (pair_send[rows_of(core)].astype(F32) + pair_recv[...].astype(F32)).astype(BF16)
    g_send[...] = dot(picks[...], both).astype(BF16).reshape(owners, PADDED, WIDTH)
    to_owners(lambda k: grad_copy(k, core * owners + k, af).start())
    lax.fori_loop(1, groups, finished, 0)

    def sent(g, carry):
        slabs_out(c_send.at[g])
        return carry

    lax.fori_loop(0, groups, sent, 0)
    for two in range(groups // 2):
        to(partner, af, h_all.at[twos], h_all.at[twos], h_send.at[two], own_sem.at[0, 0]).wait_send()
    for h in range(hours_dev):
        halo_right(h).wait_send()
        halo_left(h).wait_send()

    def count_waits(held_back, act):
        @pl.when(holds)
        def _():
            act(held_back - 1)

        @pl.when(jnp.logical_not(holds))
        def _():
            act(held_back)

    @pl.when(holds)
    def _():
        g_recv[af] = g_send[lax.rem(af, owners)]
        arrived = g_recv.at[pl.ds(0, n_af - 1)]
        to(partner, af, arrived, arrived, pair_sem.at[0], gr_sem.at[0]).wait_recv()
        t_send[...] = jnp.sum(g_recv[...].astype(F32), axis=0)
        others(n_ta, ta, lambda p: total_copy(p, ta // 2).start())
        t_recv[ta // 2] = t_send[...]

    def out_waits(g, carry):
        slabs_in(o_recv.at[g])
        slabs_out(o_send.at[g])
        own_out(g).wait()
        return carry

    pair_copy.wait_send()

    def terms_sent(count):
        sent_terms = g_send.at[pl.ds(0, count)]
        to(partner, af, sent_terms, sent_terms, gs_sem.at[0], pair_sem.at[1]).wait_send()

    count_waits(owners, terms_sent)
    lax.fori_loop(0, groups, out_waits, 0)

    def totals_in(count):
        totals = t_recv.at[pl.ds(0, count)]
        to(partner, af, totals, totals, pair_sem.at[0], tr_sem.at[0]).wait_recv()

    count_waits(n_ta // 2, totals_in)
    grad_ref[...] = jnp.sum(t_recv[...], axis=0)[:OWNED]

    @pl.when(holds)
    def _():
        sent_rows = g_total.at[pl.ds(0, (n_ta - 1) * PADDED)]
        to(partner, af, sent_rows, sent_rows, ts_sem.at[0], pair_sem.at[1]).wait_send()


def shards(n_ta, n_af, features, ws, wso, wt, wto, gain_s, gain_t, neighbours, degrees, cotangent):
    hours_dev, nodes_dev, width = features.shape
    part = nodes_dev // n_ta
    hours = hours_dev * n_ta
    groups = part // GROUP
    extended = nodes_dev + 2 * RIM
    vmem = pl.BlockSpec(memory_space=pltpu.VMEM)
    anywhere = pl.BlockSpec(memory_space=pl.ANY)
    dma = pltpu.SemaphoreType.DMA
    return pl.pallas_call(
        functools.partial(kernel, n_ta, n_af, hours * nodes_dev * n_af),
        out_shape=(
            jax.ShapeDtypeStruct(features.shape, BF16),
            jax.ShapeDtypeStruct((width // n_af, width), F32),
        ),
        in_specs=[anywhere] * 10,
        out_specs=(anywhere, vmem),
        scratch_shapes=[
            *(pltpu.VMEM(a.shape, a.dtype) for a in (features, ws, wso, wt, wto, gain_s, gain_t)),
            pltpu.SMEM(neighbours.shape, jnp.int32),
            pltpu.SMEM(degrees.shape, jnp.int32),
            pltpu.VMEM((hours_dev, 2, RIM, width), BF16),
            pltpu.VMEM((hours_dev, extended, width), BF16),
            pltpu.VMEM((hours_dev, PAIRS, BLOCK, 2 * nodes_dev), BF16),
            pltpu.VMEM((hours_dev, HEADS, HEAD + PADDED, extended), BF16),
            pltpu.VMEM((2, width, width), BF16),
            pltpu.VMEM((2, width, width), BF16),
            pltpu.VMEM((hours_dev, groups, BLOCK, width), BF16),
            pltpu.VMEM((hours, groups, GROUP, width), BF16),
            pltpu.VMEM((hours, part, width), BF16),
            pltpu.VMEM((groups, hours * GROUP, width), BF16),
            pltpu.VMEM((BLOCK, 2 * BLOCK), F32),
            pltpu.VMEM((n_af // 2 * PADDED, n_af // 2 * OWNED), BF16),
            pltpu.VMEM((hours, part, width), BF16),
            pltpu.VMEM((width, width), F32),
            pltpu.VMEM((width, width), BF16),
            pltpu.VMEM((width // 2, width), BF16),
            pltpu.VMEM((n_af // 2, PADDED, width), BF16),
            pltpu.VMEM((n_af, PADDED, width), BF16),
            pltpu.VMEM((PADDED, width), F32),
            pltpu.VMEM((n_ta // 2, PADDED, width), F32),
            dma((hours_dev, 2)),
            dma((hours_dev, 2)),
            dma((groups,)),
            dma((groups,)),
            dma((groups // 2,)),
            dma((groups // 2,)),
            dma((groups,)),
            dma((groups,)),
            dma((2,)),
            dma((1,)),
            dma((1,)),
            dma((1,)),
            dma((1,)),
            dma((2, groups)),
            dma((9,)),
        ],
        compiler_params=pltpu.CompilerParams(
            collective_id=0, has_side_effects=True, vmem_limit_bytes=63 * 2**20
        ),
    )(features, ws, wso, wt, wto, gain_s, gain_t, neighbours, degrees, cotangent)


def solution(mesh):
    return jax.shard_map(
        functools.partial(shards, mesh.shape["ta"], mesh.shape["af"]),
        mesh=mesh,
        in_specs=(
            P("ta", "af", None),
            P(),
            P(),
            P(),
            P(),
            P(),
            P(),
            P("af", None),
            P("af"),
            P("ta", "af", None),
        ),
        out_specs=(P("ta", "af", None), P("af", None)),
        check_vma=False,
    )
```
